32 devices in a mesh: gx: 8 (over z, x), gy: 4 (over y, core).
Axes of the slice: x: 2, y: 2, z: 4, core: 2. Of those that a mesh axis runs over, the one named last changes fastest.
Arguments:
- rhs: float32 [32, 32, 512], P('gx', 'gy'), may hold values from -6 to 6
- alpha: float32 [32, 32, 512], P('gx', 'gy'), may hold values from 0.0001 to 4
- beta_x: float32 [32, 32, 512], P('gx', 'gy'), may hold values from 0.5 to 2
- beta_y: float32 [32, 32, 512], P('gx', 'gy'), may hold values from 0.5 to 2
- beta_z: float32 [32, 32, 512], P('gx', 'gy'), may hold values from 0.5 to 2
Outputs:
- fine_solution: float32 [32, 32, 512], P('gx', 'gy')
- coarse_correction: float32 [8, 8, 128], P('gx', 'gy')
The draws below stay inside these ranges and needn't reach their ends.
All inputs are finite; a program needn't handle non-finite values.
Results may differ from the reference program's by a relative error of at most 0.00002.
Values sent between devices are 32-bit elements; how exact they have to be, the bound alone decides.
A program may use at most 64 MiB of HBM per device.

```python
import math
import jax
import jax.numpy as jnp
from jax import lax

SWEEPS = 4
COARSE_SWEEPS = 8
NX = 32
NY = 32
NZ = 512


def draw_rhs(key, part):
    shape = (NX, NY, NZ)
    values = jnp.clip(2.0 * jax.random.normal(key, shape, jnp.float32), -6.0, 6.0)
    return values.astype(jnp.float32)


def draw_alpha(key, part):
    shape = (NX, NY, NZ)
    key_low, key_high, key_pick = jax.random.split(key, 3)
    background = jnp.exp(jax.random.uniform(key_low, shape, jnp.float32, math.log(0.0001), math.log(0.001)))
    stiff = jnp.exp(jax.random.uniform(key_high, shape, jnp.float32, 0.0, math.log(4.0)))
    picked = jax.random.uniform(key_pick, shape, jnp.float32) < 1.0 / 2048.0
    return jnp.where(picked, stiff, background).astype(jnp.float32)


def steps_of(own_key, dims, pieces, smallest, top_value):
    factor_of, own = 1.0, jax.random.fold_in(own_key, 6)
    for dim, blocks in pieces:
        steps = jnp.exp(jax.random.uniform(jax.random.fold_in(own, dim), (blocks,), jnp.float32, smallest / len(pieces), top_value / len(pieces)))
        factor_of = factor_of * jnp.repeat(steps, dims[dim] // blocks).reshape([-1 if axis == dim else 1 for axis in range(len(dims))])
    return factor_of


def setup_inputs(seed: int = 0) -> dict:
    seeds = jax.random.split(jax.random.key(seed), 6)
    return {
        "rhs": draw_rhs(jax.random.fold_in(seeds[5], 71), 0),
        "alpha": draw_alpha(jax.random.fold_in(seeds[5], 71), 0),
        "beta_x": jnp.clip(jnp.exp(math.log(2.0) - 1.3862944 * jax.random.uniform(seeds[2], (NX, NY, NZ), jnp.float32) ** steps_of(seeds[2], (NX, NY, NZ), ((0, 8), (1, 4)), -0.2, 0.2)), 0.5, 2.0),
        "beta_y": jnp.clip(jnp.exp(math.log(2.0) - 1.3862944 * jax.random.uniform(seeds[3], (NX, NY, NZ), jnp.float32) ** steps_of(seeds[3], (NX, NY, NZ), ((0, 8), (1, 4)), -0.2, 0.2)), 0.5, 2.0),
        "beta_z": jnp.clip(jnp.exp(math.log(2.0) - 1.3862944 * jax.random.uniform(seeds[4], (NX, NY, NZ), jnp.float32) ** steps_of(seeds[4], (NX, NY, NZ), ((0, 8), (1, 4)), -0.2, 0.2)), 0.5, 2.0),
    }


def upper_faces(beta, axis_pos):
    rest = lax.slice_in_dim(beta, 1, beta.shape[axis_pos], axis=axis_pos)
    zero_layer = jnp.zeros_like(lax.slice_in_dim(beta, 0, 1, axis=axis_pos))
    return jnp.concatenate([rest, zero_layer], axis=axis_pos)


def coarsen_face(faces, axis_pos, upper):
    size_x, size_y, size_z = faces.shape
    blocks = faces.reshape(size_x // 2, 2, size_y // 2, 2, size_z // 2, 2)
    taken = 2 * axis_pos + 1
    picked = jnp.take(blocks, upper, axis=taken)
    others = tuple(pair - 1 if pair > taken else pair for pair in (1, 3, 5) if pair != taken)
    return jnp.mean(picked, axis=others) * 0.25


def coarsen_all(faces):
    return tuple(coarsen_face(faces[number], number // 2, number % 2) for number in range(6))


def restrict(field):
    size_x, size_y, size_z = field.shape
    return jnp.mean(field.reshape(size_x // 2, 2, size_y // 2, 2, size_z // 2, 2), axis=(1, 3, 5))


def prolong(field):
    return jnp.repeat(jnp.repeat(jnp.repeat(field, 2, 0), 2, 1), 2, 2)


def beside_sum(padded, faces):
    total = faces[0] * padded[:-2, 1:-1, 1:-1] + faces[1] * padded[2:, 1:-1, 1:-1]
    total = total + faces[2] * padded[1:-1, :-2, 1:-1] + faces[3] * padded[1:-1, 2:, 1:-1]
    total = total + faces[4] * padded[1:-1, 1:-1, :-2] + faces[5] * padded[1:-1, 1:-1, 2:]
    return total


def diagonal_of(cell_coef, faces):
    total = cell_coef
    for face in faces:
        total = total + face
    return total


def red_cells(shape, offset_x, offset_y):
    index_x = jnp.arange(shape[0], dtype=jnp.int32) + offset_x
    index_y = jnp.arange(shape[1], dtype=jnp.int32) + offset_y
    index_z = jnp.arange(shape[2], dtype=jnp.int32)
    return (index_x[:, None, None] + index_y[None, :, None] + index_z[None, None, :]) % 2 == 0


def smooth(field, source, inverse, faces, red_mask, count):
    for sweep_index in range(count):
        for colour in (True, False):
            beside = beside_sum(jnp.pad(field, 1), faces)
            field = jnp.where(red_mask == colour, (source + beside) * inverse, field)
    return field


def residual_of(field, source, diagonal, faces):
    return source - (diagonal * field - beside_sum(jnp.pad(field, 1), faces))


def reference(rhs, alpha, beta_x, beta_y, beta_z):
    faces_fine = (beta_x, upper_faces(beta_x, 0), beta_y, upper_faces(beta_y, 1), beta_z, upper_faces(beta_z, 2))
    diagonal_fine = diagonal_of(alpha, faces_fine)
    smoothed = smooth(jnp.zeros_like(rhs), rhs, 1.0 / diagonal_fine, faces_fine, red_cells(rhs.shape, 0, 0), SWEEPS)
    source_mid = restrict(residual_of(smoothed, rhs, diagonal_fine, faces_fine))
    coef_mid = restrict(alpha)
    faces_mid = coarsen_all(faces_fine)
    diagonal_mid = diagonal_of(coef_mid, faces_mid)
    level_mid = smooth(jnp.zeros_like(source_mid), source_mid, 1.0 / diagonal_mid, faces_mid, red_cells(source_mid.shape, 0, 0), SWEEPS)
    source_low = restrict(residual_of(level_mid, source_mid, diagonal_mid, faces_mid))
    coef_low = restrict(coef_mid)
    faces_low = coarsen_all(faces_mid)
    inverse_low = 1.0 / diagonal_of(coef_low, faces_low)
    coarse = smooth(jnp.zeros_like(source_low), source_low, inverse_low, faces_low, red_cells(source_low.shape, 0, 0), COARSE_SWEEPS)
    corrected = level_mid + prolong(coarse)
    return smoothed + prolong(corrected), coarse
```

```python
import functools

import jax
import jax.numpy as jnp
from jax import lax
from jax.experimental import pallas as pl
from jax.experimental.pallas import tpu as pltpu
from jax.sharding import PartitionSpec as P

SWEEPS = 4
COARSE_SWEEPS = 8
MESH = pl.DeviceIdType.MESH
F32 = jnp.float32
LANES = 128


def order_matrix(size, back):
    quarter = size // 4
    row = lax.broadcasted_iota(jnp.int32, (size, size), 1 if back else 0)
    col = lax.broadcasted_iota(jnp.int32, (size, size), 0 if back else 1)
    hit = row == 4 * (col % quarter) + col // quarter
    return jnp.where(hit, 1.0, 0.0).astype(jnp.bfloat16)


def permuted(rows, matrix):
    count = rows.shape[0]
    high = rows.astype(jnp.bfloat16)
    rest = rows - high.astype(F32)
    middle = rest.astype(jnp.bfloat16)
    low = (rest - middle.astype(F32)).astype(jnp.bfloat16)
    stacked = jnp.concatenate([high, middle, low], 0)
    out = jnp.dot(stacked, matrix, preferred_element_type=F32)
    return (out[2 * count :] + out[count : 2 * count]) + out[:count]


def kernel(
    ngx, ngy,
    rhs_ref, alpha_ref, bx_ref, by_ref, bz_ref,
    fine_ref, coarse_ref,
    l0, v0, hx, ys, hy, pairs, src_all, coef_all, l1, wx1, v1, c2, spread,
    xsend, xrecv, ysend, yrecv, gsend, grecv, csend, crecv,
):
    gx = lax.axis_index("gx")
    gy = lax.axis_index("gy")
    size_x, size_y, size_z = rhs_ref.shape
    quarter = size_z // 4
    own_p = size_y // 4
    shape0 = (size_x, 4, size_y, quarter)

    hx[...] = jnp.zeros(hx.shape, F32)
    hy[...] = jnp.zeros(hy.shape, F32)

    barrier = pltpu.get_barrier_semaphore()

    def greet_x(step, carry):
        other = lax.rem(gx + step, ngx)
        pl.semaphore_signal(barrier, inc=1, device_id=(other, gy), device_id_type=MESH)
        return carry

    def greet_y(step, carry):
        other = lax.rem(gy + step, ngy)
        pl.semaphore_signal(barrier, inc=1, device_id=(gx, other), device_id_type=MESH)
        return carry

    lax.fori_loop(1, ngx, greet_x, 0)
    lax.fori_loop(1, ngy, greet_y, 0)

    matrix = order_matrix(size_z, False)
    rows = size_x * size_y
    stacked = jnp.concatenate(
        [ref[...].reshape(rows, size_z) for ref in (rhs_ref, alpha_ref, bx_ref, by_ref, bz_ref)], 0
    )
    ordered = permuted(stacked, matrix)

    def ordered_field(number):
        whole = ordered[number * rows : (number + 1) * rows].reshape(size_x, size_y, size_z)
        return jnp.stack([whole[:, :, r * quarter : (r + 1) * quarter] for r in range(4)], 1)

    rhs, alpha, bx, by, bz = [ordered_field(number) for number in range(5)]
    RHS, INV, DIAG, WXL, WXU, WYL, WYU, WZL, WZU = range(9)
    l0[RHS] = rhs
    l0[WXL] = bx
    l0[WYL] = by

    pl.semaphore_wait(barrier, ngx - 1 + ngy - 1)

    def x_copy(slot, up, source):
        side = 0 if up else 1
        return pltpu.make_async_remote_copy(
            src_ref=source,
            dst_ref=hx.at[slot, side],
            send_sem=xsend.at[slot, side],
            recv_sem=xrecv.at[slot, side],
            device_id=(gx + 1 if up else gx - 1, gy),
            device_id_type=MESH,
        )

    def y_copy(slot, up):
        side = 0 if up else 1
        return pltpu.make_async_remote_copy(
            src_ref=ys.at[slot, side],
            dst_ref=hy.at[slot, side],
            send_sem=ysend.at[slot, side],
            recv_sem=yrecv.at[slot, side],
            device_id=(gx, gy + 1 if up else gy - 1),
            device_id_type=MESH,
        )

    has_low_x, has_high_x = gx > 0, gx < ngx - 1
    has_low_y, has_high_y = gy > 0, gy < ngy - 1

    def start_exchange(slot, field, ups=(False, True)):
        for up in ups:
            @pl.when(has_high_x if up else has_low_x)
            def _():
                x_copy(slot, up, field.at[size_x - 1 if up else 0]).start()
        for up in ups:
            @pl.when(has_high_y if up else has_low_y)
            def _():
                y_copy(slot, up).start()

    def end_exchange(slot, field, ups=(False, True)):
        for up in ups:
            @pl.when(has_low_x if up else has_high_x)
            def _():
                x_copy(slot, up, field.at[size_x - 1 if up else 0]).wait_recv()
        for up in ups:
            @pl.when(has_low_y if up else has_high_y)
            def _():
                y_copy(slot, up).wait_recv()
        for up in ups:
            @pl.when(has_high_x if up else has_low_x)
            def _():
                x_copy(slot, up, field.at[size_x - 1 if up else 0]).wait_send()
        for up in ups:
            @pl.when(has_high_y if up else has_low_y)
            def _():
                y_copy(slot, up).wait_send()

    ys[0, 1] = by[:, :, 0:1]
    start_exchange(0, l0.at[WXL], (False,))

    def pair_x(field):
        grouped = field.reshape(size_x // 2, 2, *field.shape[1:])
        return grouped[:, 0] + grouped[:, 1]

    def first_x(field):
        return field.reshape(size_x // 2, 2, *field.shape[1:])[:, 0]

    def pair_z(field):
        return jnp.stack([field[:, 0] + field[:, 1], field[:, 2] + field[:, 3]], 1)

    def first_z(field):
        return jnp.stack([field[:, 0], field[:, 2]], 1)

    def packed(field, pair_y):
        if pair_y:
            field = field + pltpu.roll(field, size_y - 1, 2)
        pairs[...] = field
        even = pairs[:, :, pl.ds(0, own_p, stride=4), :]
        odd = pairs[:, :, pl.ds(2, own_p, stride=4), :]
        return even, odd

    def put(ref, field, pair_y, scale):
        even, odd = packed(field * scale, pair_y)
        ref[:, :, 0] = even
        ref[:, :, 1] = odd

    put(coef_all.at[gy, gx, 0], pair_z(pair_x(alpha)), True, 0.125)
    put(coef_all.at[gy, gx, 1], pair_z(first_x(bx)), True, 0.0625)
    put(coef_all.at[gy, gx, 2], pair_z(pair_x(by)), False, 0.0625)
    put(coef_all.at[gy, gx, 3], first_z(pair_x(bz)), True, 0.0625)

    def row_copy(ref, ssem, rsem, other, slot):
        return pltpu.make_async_remote_copy(
            src_ref=ref.at[gy, gx], dst_ref=ref.at[gy, slot],
            send_sem=ssem.at[0, other], recv_sem=rsem.at[0, slot],
            device_id=(other, gy), device_id_type=MESH,
        )

    def column_copy(ref, ssem, rsem, other, slot):
        return pltpu.make_async_remote_copy(
            src_ref=ref.at[gy], dst_ref=ref.at[slot],
            send_sem=ssem.at[1, other], recv_sem=rsem.at[1, slot],
            device_id=(gx, other), device_id_type=MESH,
        )

    def each_other(count, me, action):
        def step(number, carry):
            action(lax.rem(me + number, count))
            return carry

        lax.fori_loop(1, count, step, 0)

    def row_start(ref, ssem, rsem):
        each_other(ngx, gx, lambda other: row_copy(ref, ssem, rsem, other, gx).start())

    def row_wait(ref, ssem, rsem):
        each_other(ngx, gx, lambda other: row_copy(ref, ssem, rsem, other, other).wait_recv())
        each_other(ngx, gx, lambda other: row_copy(ref, ssem, rsem, other, gx).wait_send())

    def column_start(ref, ssem, rsem):
        each_other(ngy, gy, lambda other: column_copy(ref, ssem, rsem, other, gy).start())

    def column_wait(ref, ssem, rsem):
        each_other(ngy, gy, lambda other: column_copy(ref, ssem, rsem, other, other).wait_recv())
        each_other(ngy, gy, lambda other: column_copy(ref, ssem, rsem, other, gy).wait_send())

    row_y = lax.broadcasted_iota(jnp.int32, shape0, 2)
    lane = lax.broadcasted_iota(jnp.int32, shape0, 3)
    residue = lax.broadcasted_iota(jnp.int32, shape0, 1)
    row_x = lax.broadcasted_iota(jnp.int32, shape0, 0)
    offset = gx * size_x + gy * size_y
    red0 = (row_x + residue + row_y + offset) % 2 == 0

    def z_lower(field):
        return jnp.concatenate([pltpu.roll(field[:, 3:], 1, 3), field[:, :3]], 1)

    def z_upper(field):
        return jnp.concatenate([field[:, 1:], pltpu.roll(field[:, :1], quarter - 1, 3)], 1)

    wzu = jnp.where((residue == 3) & (lane == quarter - 1), 0.0, z_upper(bz))
    l0[WZU] = wzu
    l0[WZL] = jnp.where((residue == 0) & (lane == 0), 0.0, bz)

    end_exchange(0, l0.at[WXL], (False,))
    row_start(coef_all, csend, crecv)
    wxu = jnp.concatenate([bx[1:], hx[0, 1][None]], 0)
    wyu = jnp.where(row_y == size_y - 1, hy[0, 1], pltpu.roll(by, size_y - 1, 2))
    l0[WXU] = wxu
    l0[WYU] = wyu
    diagonal = alpha + bx + wxu + by + wyu + bz + wzu
    l0[DIAG] = diagonal
    inverse = 1.0 / diagonal
    l0[INV] = inverse

    def beside0(slot):
        field = v0[...]
        below_x = jnp.concatenate([hx[slot, 0][None], field[:-1]], 0)
        above_x = jnp.concatenate([field[1:], hx[slot, 1][None]], 0)
        below_y = jnp.where(row_y == 0, hy[slot, 0], pltpu.roll(field, 1, 2))
        above_y = jnp.where(row_y == size_y - 1, hy[slot, 1], pltpu.roll(field, size_y - 1, 2))
        total = l0[WXL] * below_x + l0[WXU] * above_x
        total = total + (l0[WYL] * below_y + l0[WYU] * above_y)
        return total + (l0[WZL] * z_lower(field) + l0[WZU] * z_upper(field))

    def publish(slot, field):
        v0[...] = field
        ys[slot, 0] = field[:, :, size_y - 1 :]
        ys[slot, 1] = field[:, :, 0:1]
        start_exchange(slot, v0)

    publish(1, jnp.where(red0, rhs * inverse, 0.0))
    for half in range(1, 2 * SWEEPS):
        slot = half % 2
        end_exchange(slot, v0)
        updated = (l0[RHS] + beside0(slot)) * l0[INV]
        mask = red0 if half % 2 == 0 else jnp.logical_not(red0)
        publish(1 - slot, jnp.where(mask, updated, v0[...]))
        if half == 3:
            row_wait(coef_all, csend, crecv)
            column_start(coef_all, csend, crecv)
    end_exchange(0, v0)
    residual0 = l0[RHS] - (l0[DIAG] * v0[...] - beside0(0))
    put(src_all.at[gy, gx], pair_z(pair_x(residual0)), True, 0.125)
    row_start(src_all, gsend, grecv)
    column_wait(coef_all, csend, crecv)

    size_p = own_p * ngy
    shape1 = (ngx, 2, 2, 2, size_p, quarter)
    S1, INV1, DIAG1, WYL1, WZL1, UPPER1 = range(6)

    def whole_field(ref, number, block):
        parts = []
        for j in range(ngy):
            parts.append(ref[j, block] if number is None else ref[j, block, number])
        return jnp.concatenate(parts, 3)

    wx1[ngx] = jnp.zeros(shape1[1:], F32)
    v1[...] = jnp.zeros(v1.shape, F32)
    row_p = lax.broadcasted_iota(jnp.int32, shape1[2:], 2)
    lane1 = lax.broadcasted_iota(jnp.int32, shape1[2:], 3)
    half_r = lax.broadcasted_iota(jnp.int32, shape1[2:], 0)
    half_s = lax.broadcasted_iota(jnp.int32, shape1[2:], 1)

    def coefs(block, carry):
        wx1[block] = whole_field(coef_all, 1, block)
        return carry

    lax.fori_loop(0, ngx, coefs, 0)

    def more_coefs(block, carry):
        a1 = whole_field(coef_all, 0, block)
        lower_x = wx1[block]
        next_x = wx1[block + 1]
        upper_x = jnp.stack([lower_x[1], next_x[0]], 0)
        lower_y = whole_field(coef_all, 2, block)
        upper_y = jnp.stack([lower_y[:, :, 1], pltpu.roll(lower_y[:, :, 0], size_p - 1, 2)], 2)
        upper_y = jnp.where((half_s == 1) & (row_p == size_p - 1), 0.0, upper_y)
        lower_z = whole_field(coef_all, 3, block)
        upper_z = jnp.stack([lower_z[:, 1], pltpu.roll(lower_z[:, 0], quarter - 1, 3)], 1)
        upper_z = jnp.where((half_r == 1) & (lane1 == quarter - 1), 0.0, upper_z)
        diagonal1 = a1 + lower_x + upper_x + lower_y + upper_y + lower_z + upper_z
        l1[DIAG1, block] = diagonal1
        l1[INV1, block] = 1.0 / diagonal1
        l1[WYL1, block] = lower_y
        l1[UPPER1, block, :, 0] = upper_y[:, :, 1]
        l1[WZL1, block] = lower_z
        l1[UPPER1, block, :, 1] = upper_z[:, 1]
        return carry

    lax.fori_loop(0, ngx, more_coefs, 0)

    shape2 = (ngx, size_p, quarter)
    row2 = lax.broadcasted_iota(jnp.int32, shape2, 1)
    lane2 = lax.broadcasted_iota(jnp.int32, shape2, 2)
    block2 = lax.broadcasted_iota(jnp.int32, shape2, 0)
    red2 = (block2 + row2 + lane2) % 2 == 0

    def summed(ref, fixed):
        total = None
        for xl in (0, 1):
            for r in (0, 1):
                for s in (0, 1):
                    if (xl, r, s)[fixed] == 0:
                        term = ref(xl, r, s)
                        total = term if total is None else total + term
        return total

    a2_parts = None
    for j in range(ngy):
        part = None
        for xl in (0, 1):
            for r in (0, 1):
                for s in (0, 1):
                    term = coef_all[j, :, 0, xl, r, s]
                    part = term if part is None else part + term
        a2_parts = [part] if a2_parts is None else a2_parts + [part]
    a2 = jnp.concatenate(a2_parts, 1) * 0.125
    lower_x2 = summed(lambda xl, r, s: wx1[0:ngx, xl, r, s], 0) * 0.0625
    lower_y2 = summed(lambda xl, r, s: l1[WYL1, :, xl, r, s], 2) * 0.0625
    lower_z2 = summed(lambda xl, r, s: l1[WZL1, :, xl, r, s], 1) * 0.0625
    upper_x2 = jnp.concatenate([lower_x2[1:], jnp.zeros((1, size_p, quarter), F32)], 0)
    upper_y2 = jnp.where(row2 == size_p - 1, 0.0, pltpu.roll(lower_y2, size_p - 1, 1))
    upper_z2 = jnp.where(lane2 == quarter - 1, 0.0, pltpu.roll(lower_z2, quarter - 1, 2))
    diagonal2 = a2 + lower_x2 + upper_x2 + lower_y2 + upper_y2 + lower_z2 + upper_z2
    A2, WXL2, WXU2, WYL2, WYU2, WZL2, WZU2 = range(7)
    c2[A2] = 1.0 / diagonal2
    c2[WXL2] = lower_x2
    c2[WXU2] = upper_x2
    c2[WYL2] = jnp.where(row2 == 0, 0.0, lower_y2)
    c2[WYU2] = upper_y2
    c2[WZL2] = jnp.where(lane2 == 0, 0.0, lower_z2)
    c2[WZU2] = upper_z2
    for xl in (0, 1):
        for r in (0, 1):
            l1[WYL1, :, xl, r, 0] = jnp.where(row2 == 0, 0.0, l1[WYL1, :, xl, r, 0])
        for s in (0, 1):
            l1[WZL1, :, xl, 0, s] = jnp.where(lane2 == 0, 0.0, l1[WZL1, :, xl, 0, s])

    row_wait(src_all, gsend, grecv)
    column_start(src_all, gsend, grecv)
    column_wait(src_all, gsend, grecv)

    for block in range(ngx):
        l1[S1, block] = whole_field(src_all, None, block)

    def beside1(xl, r, s):
        if xl == 0:
            below_x = v1[0:ngx, 1, r, s]
            above_x = v1[1 : ngx + 1, 1, r, s]
            face_above = wx1[0:ngx, 1, r, s]
        else:
            below_x = v1[1 : ngx + 1, 0, r, s]
            above_x = v1[2 : ngx + 2, 0, r, s]
            face_above = wx1[1 : ngx + 1, 0, r, s]
        side_y = v1[1 : ngx + 1, xl, r, 1 - s]
        side_z = v1[1 : ngx + 1, xl, 1 - r, s]
        below_y = pltpu.roll(side_y, 1, 1) if s == 0 else side_y
        above_y = side_y if s == 0 else pltpu.roll(side_y, size_p - 1, 1)
        below_z = pltpu.roll(side_z, 1, 2) if r == 0 else side_z
        above_z = side_z if r == 0 else pltpu.roll(side_z, quarter - 1, 2)
        total = wx1[0:ngx, xl, r, s] * below_x + face_above * above_x
        upper_y = l1[WYL1, :, xl, r, 1] if s == 0 else l1[UPPER1, :, xl, 0, r]
        upper_z = l1[WZL1, :, xl, 1, s] if r == 0 else l1[UPPER1, :, xl, 1, s]
        total = total + (l1[WYL1, :, xl, r, s] * below_y + upper_y * above_y)
        return total + (l1[WZL1, :, xl, r, s] * below_z + upper_z * above_z)

    def half1(colour):
        for xl in (0, 1):
            for r in (0, 1):
                s = (xl + r + colour) % 2
                v1[1 : ngx + 1, xl, r, s] = (
                    l1[S1, :, xl, r, s] + beside1(xl, r, s)
                ) * l1[INV1, :, xl, r, s]

    def sweep1(number, carry):
        half1(0)
        half1(1)
        return carry

    lax.fori_loop(0, SWEEPS, sweep1, 0)

    source2 = None
    for xl in (0, 1):
        for r in (0, 1):
            for s in (0, 1):
                term = l1[S1, :, xl, r, s] - (
                    l1[DIAG1, :, xl, r, s] * v1[1 : ngx + 1, xl, r, s] - beside1(xl, r, s)
                )
                source2 = term if source2 is None else source2 + term
    source2 = source2 * 0.125

    zero_block = jnp.zeros((1, size_p, quarter), F32)

    def half2(field, mask):
        below_x = jnp.concatenate([zero_block, field[:-1]], 0)
        above_x = jnp.concatenate([field[1:], zero_block], 0)
        total = c2[WXL2] * below_x + c2[WXU2] * above_x
        total = total + (
            c2[WYL2] * pltpu.roll(field, 1, 1) + c2[WYU2] * pltpu.roll(field, size_p - 1, 1)
        )
        total = total + (
            c2[WZL2] * pltpu.roll(field, 1, 2) + c2[WZU2] * pltpu.roll(field, quarter - 1, 2)
        )
        return jnp.where(mask, (source2 + total) * c2[A2], field)

    def sweep2(number, field):
        return half2(half2(field, red2), jnp.logical_not(red2))

    coarse = lax.fori_loop(0, COARSE_SWEEPS, sweep2, jnp.zeros(shape2, F32))
    c2[A2] = coarse

    shift = lax.rem(size_p - own_p * gy, size_p)
    own_coarse = c2[A2, gx]
    coarse_ref[0] = pltpu.roll(own_coarse, shift, 0)[:own_p]
    for xl in (0, 1):
        for r in (0, 1):
            for s in (0, 1):
                tile = pltpu.roll(v1[gx + 1, xl, r, s] + own_coarse, shift, 0)[:own_p]
                spread[xl, r, pl.ds(2 * s, own_p, stride=4), :] = tile
                spread[xl, r, pl.ds(2 * s + 1, own_p, stride=4), :] = tile
    added = []
    for x in range(size_x):
        added.append(jnp.concatenate([v0[x, r] + spread[x // 2, r // 2] for r in range(4)], 1))
    natural = permuted(jnp.concatenate(added, 0), order_matrix(size_z, True))
    fine_ref[...] = natural.reshape(size_x, size_y, size_z)


def on_device(ngx, ngy, rhs, alpha, beta_x, beta_y, beta_z):
    size_x, size_y, size_z = rhs.shape
    quarter = size_z // 4
    own_p = size_y // 4
    size_p = own_p * ngy
    field0 = (size_x, 4, size_y, quarter)
    block1 = (2, 2, 2, size_p, quarter)
    piece1 = (2, 2, 2, own_p, quarter)
    dma = pltpu.SemaphoreType.DMA
    most = max(ngx, ngy)
    return pl.pallas_call(
        functools.partial(kernel, ngx, ngy),
        out_shape=(
            jax.ShapeDtypeStruct(rhs.shape, F32),
            jax.ShapeDtypeStruct((size_x // 4, own_p, quarter), F32),
        ),
        in_specs=[pl.BlockSpec(memory_space=pltpu.VMEM)] * 5,
        out_specs=(pl.BlockSpec(memory_space=pltpu.VMEM),) * 2,
        scratch_shapes=[
            pltpu.VMEM((9,) + field0, F32),
            pltpu.VMEM(field0, F32),
            pltpu.VMEM((2, 2) + field0[1:], F32),
            pltpu.VMEM((2, 2, size_x, 4, 1, quarter), F32),
            pltpu.VMEM((2, 2, size_x, 4, 1, quarter), F32),
            pltpu.VMEM((size_x // 2, 2, size_y, quarter), F32),
            pltpu.VMEM((ngy, ngx) + piece1, F32),
            pltpu.VMEM((ngy, ngx, 4) + piece1, F32),
            pltpu.VMEM((6, ngx) + block1, F32),
            pltpu.VMEM((ngx + 1,) + block1, F32),
            pltpu.VMEM((ngx + 2,) + block1, F32),
            pltpu.VMEM((7, ngx, size_p, quarter), F32),
            pltpu.VMEM((2, 2, size_y, quarter), F32),
            dma((2, 2)), dma((2, 2)), dma((2, 2)), dma((2, 2)),
            dma((2, most)), dma((2, most)), dma((2, most)), dma((2, most)),
        ],
        compiler_params=pltpu.CompilerParams(
            collective_id=0, has_side_effects=True, vmem_limit_bytes=62 * 1024 * 1024
        ),
    )(rhs, alpha, beta_x, beta_y, beta_z)


def solution(mesh):
    spec = P("gx", "gy", None)
    return jax.shard_map(
        functools.partial(on_device, mesh.shape["gx"], mesh.shape["gy"]),
        mesh=mesh,
        in_specs=(spec,) * 5,
        out_specs=(spec, spec),
        check_vma=False,
    )
```

```python
import functools

import jax
import jax.numpy as jnp
from jax import lax
from jax.experimental import pallas as pl
from jax.experimental.pallas import tpu as pltpu
from jax.sharding import PartitionSpec as P

SWEEPS = 4
COARSE_SWEEPS = 8
MESH = pl.DeviceIdType.MESH
F32 = jnp.float32
LANES = 128


def order_matrix(size, back):
    quarter = size // 4
    row = lax.broadcasted_iota(jnp.int32, (size, size), 1 if back else 0)
    col = lax.broadcasted_iota(jnp.int32, (size, size), 0 if back else 1)
    hit = row == 4 * (col % quarter) + col // quarter
    return jnp.where(hit, 1.0, 0.0).astype(jnp.bfloat16)


def permuted(rows, matrix):
    count = rows.shape[0]
    high = rows.astype(jnp.bfloat16)
    rest = rows - high.astype(F32)
    middle = rest.astype(jnp.bfloat16)
    low = (rest - middle.astype(F32)).astype(jnp.bfloat16)
    stacked = jnp.concatenate([high, middle, low], 0)
    out = jnp.dot(stacked, matrix, preferred_element_type=F32)
    return (out[2 * count :] + out[count : 2 * count]) + out[:count]


def kernel(
    ngx, ngy,
    rhs_ref, alpha_ref, bx_ref, by_ref, bz_ref,
    fine_ref, coarse_ref,
    l0, v0, hx, bx_in, px, qx, ys, hy, pairs, src_all, coef_all, l1, wx1, v1, c2, spread,
    xsend, xrecv, ysend, yrecv, gsend, grecv, csend, crecv,
):
    gx = lax.axis_index("gx")
    gy = lax.axis_index("gy")
    size_x, size_y, size_z = rhs_ref.shape
    quarter = size_z // 4
    own_p = size_y // 4
    chips, chip, core = ngy // 2, gy // 2, lax.rem(gy, 2)
    column = core * chips + chip
    shape0 = (size_x, 4, size_y, quarter)

    hx[...] = jnp.zeros(hx.shape, F32)
    bx_in[...] = jnp.zeros(bx_in.shape, F32)
    hy[...] = jnp.zeros(hy.shape, F32)

    barrier = pltpu.get_barrier_semaphore()

    def greet_x(step, carry):
        other = lax.rem(gx + step, ngx)
        pl.semaphore_signal(barrier, inc=1, device_id=(other, gy), device_id_type=MESH)
        return carry

    def greet_y(step, carry):
        other = lax.rem(gy + step, ngy)
        pl.semaphore_signal(barrier, inc=1, device_id=(gx, other), device_id_type=MESH)
        return carry

    lax.fori_loop(1, ngx, greet_x, 0)
    lax.fori_loop(1, ngy, greet_y, 0)

    matrix = order_matrix(size_z, False)
    rows = size_x * size_y
    stacked = jnp.concatenate(
        [ref[...].reshape(rows, size_z) for ref in (rhs_ref, alpha_ref, bx_ref, by_ref, bz_ref)], 0
    )
    ordered = permuted(stacked, matrix)

    def ordered_field(number):
        whole = ordered[number * rows : (number + 1) * rows].reshape(size_x, size_y, size_z)
        return jnp.stack([whole[:, :, r * quarter : (r + 1) * quarter] for r in range(4)], 1)

    rhs, alpha, bx, by, bz = [ordered_field(number) for number in range(5)]
    RHS, INV, DIAG, WXL, WXU, WYL, WYU, WZL, WZU = range(9)
    l0[RHS] = rhs
    l0[WXL] = bx
    l0[WYL] = by

    pl.semaphore_wait(barrier, ngx - 1 + ngy - 1)

    def x_copy(slot, up):
        side = 0 if up else 1
        return pltpu.make_async_remote_copy(
            src_ref=px.at[slot, side],
            dst_ref=qx.at[slot, side],
            send_sem=xsend.at[slot, side],
            recv_sem=xrecv.at[slot, side],
            device_id=(gx + 1 if up else gx - 1, gy),
            device_id_type=MESH,
        )

    def y_copy(slot, up):
        side = 0 if up else 1
        return pltpu.make_async_remote_copy(
            src_ref=ys.at[slot, side],
            dst_ref=hy.at[slot, side],
            send_sem=ysend.at[slot, side],
            recv_sem=yrecv.at[slot, side],
            device_id=(gx, gy + 1 if up else gy - 1),
            device_id_type=MESH,
        )

    face_copy = pltpu.make_async_remote_copy(
        src_ref=l0.at[WXL, 0],
        dst_ref=bx_in,
        send_sem=xsend.at[2, 0],
        recv_sem=xrecv.at[2, 0],
        device_id=(gx - 1, gy),
        device_id_type=MESH,
    )

    has_low_x, has_high_x = gx > 0, gx < ngx - 1
    has_low_y, has_high_y = gy > 0, gy < ngy - 1

    def strided(colour, up, r):
        x = size_x - 1 if up else 0
        return pl.ds((colour + x + r) % 2, size_y // 2, stride=2)

    def start_exchange(slot, colour):
        for up in (False, True):
            side = 0 if up else 1
            plane = size_x - 1 if up else 0

            @pl.when(has_high_x if up else has_low_x)
            def _():
                for r in range(4):
                    px[slot, side, r] = v0[plane, r, strided(colour, up, r), :]
                x_copy(slot, up).start()
        for up in (False, True):
            @pl.when(has_high_y if up else has_low_y)
            def _():
                y_copy(slot, up).start()

    def end_exchange(slot, colour):
        for up in (False, True):
            side = 0 if up else 1

            @pl.when(has_low_y if up else has_high_y)
            def _():
                y_copy(slot, up).wait_recv()

            @pl.when(has_low_x if up else has_high_x)
            def _():
                x_copy(slot, up).wait_recv()
                for r in range(4):
                    hx[side, r, strided(colour, up, r), :] = qx[slot, side, r]

    def free_slot(slot):
        for up in (False, True):
            @pl.when(has_high_x if up else has_low_x)
            def _():
                x_copy(slot, up).wait_send()

            @pl.when(has_high_y if up else has_low_y)
            def _():
                y_copy(slot, up).wait_send()

    ys[0, 1] = by[:, :, 0:1]

    @pl.when(has_low_x)
    def _():
        face_copy.start()

    @pl.when(has_low_y)
    def _():
        y_copy(0, False).start()

    def pair_x(field):
        grouped = field.reshape(size_x // 2, 2, *field.shape[1:])
        return grouped[:, 0] + grouped[:, 1]

    def first_x(field):
        return field.reshape(size_x // 2, 2, *field.shape[1:])[:, 0]

    def pair_z(field):
        return jnp.stack([field[:, 0] + field[:, 1], field[:, 2] + field[:, 3]], 1)

    def first_z(field):
        return jnp.stack([field[:, 0], field[:, 2]], 1)

    def packed(field, pair_y):
        if pair_y:
            field = field + pltpu.roll(field, size_y - 1, 2)
        pairs[...] = field
        even = pairs[:, :, pl.ds(0, own_p, stride=4), :]
        odd = pairs[:, :, pl.ds(2, own_p, stride=4), :]
        return even, odd

    def put(ref, field, pair_y, scale):
        even, odd = packed(field * scale, pair_y)
        ref[:, :, 0] = even
        ref[:, :, 1] = odd

    put(coef_all.at[column, gx, 0], pair_z(pair_x(alpha)), True, 0.125)
    put(coef_all.at[column, gx, 1], pair_z(first_x(bx)), True, 0.0625)
    put(coef_all.at[column, gx, 2], pair_z(pair_x(by)), False, 0.0625)
    put(coef_all.at[column, gx, 3], first_z(pair_x(bz)), True, 0.0625)

    def row_copy(ref, ssem, rsem, other, slot):
        return pltpu.make_async_remote_copy(
            src_ref=ref.at[column, gx], dst_ref=ref.at[column, slot],
            send_sem=ssem.at[0, other], recv_sem=rsem.at[0, slot],
            device_id=(other, gy), device_id_type=MESH,
        )

    def column_copy(ref, ssem, rsem, other, slot):
        return pltpu.make_async_remote_copy(
            src_ref=ref.at[column], dst_ref=ref.at[core * chips + slot],
            send_sem=ssem.at[1, other], recv_sem=rsem.at[1, slot],
            device_id=(gx, 2 * other + core), device_id_type=MESH,
        )

    def core_copy(ref, ssem, rsem, slot):
        whole = ref.at[pl.ds(slot * chips, chips)]
        return pltpu.make_async_remote_copy(
            src_ref=whole, dst_ref=whole,
            send_sem=ssem.at[2, 0], recv_sem=rsem.at[2, 0],
            device_id=(gx, 2 * chip + 1 - core), device_id_type=MESH,
        )

    def each_other(count, me, action):
        def step(number, carry):
            action(lax.rem(me + number, count))
            return carry

        lax.fori_loop(1, count, step, 0)

    def row_start(ref, ssem, rsem):
        each_other(ngx, gx, lambda other: row_copy(ref, ssem, rsem, other, gx).start())

    def row_wait(ref, ssem, rsem):
        each_other(ngx, gx, lambda other: row_copy(ref, ssem, rsem, other, other).wait_recv())
        each_other(ngx, gx, lambda other: row_copy(ref, ssem, rsem, other, gx).wait_send())

    def column_start(ref, ssem, rsem):
        each_other(chips, chip, lambda other: column_copy(ref, ssem, rsem, other, chip).start())

    def column_wait(ref, ssem, rsem):
        each_other(chips, chip, lambda other: column_copy(ref, ssem, rsem, other, other).wait_recv())
        each_other(chips, chip, lambda other: column_copy(ref, ssem, rsem, other, chip).wait_send())

    row_y = lax.broadcasted_iota(jnp.int32, shape0, 2)
    lane = lax.broadcasted_iota(jnp.int32, shape0, 3)
    residue = lax.broadcasted_iota(jnp.int32, shape0, 1)
    row_x = lax.broadcasted_iota(jnp.int32, shape0, 0)
    offset = gx * size_x + gy * size_y
    red0 = (row_x + residue + row_y + offset) % 2 == 0

    def z_lower(field):
        return jnp.concatenate([pltpu.roll(field[:, 3:], 1, 3), field[:, :3]], 1)

    def z_upper(field):
        return jnp.concatenate([field[:, 1:], pltpu.roll(field[:, :1], quarter - 1, 3)], 1)

    wzu = jnp.where((residue == 3) & (lane == quarter - 1), 0.0, z_upper(bz))
    l0[WZU] = wzu
    l0[WZL] = jnp.where((residue == 0) & (lane == 0), 0.0, bz)

    @pl.when(has_high_x)
    def _():
        face_copy.wait_recv()

    @pl.when(has_high_y)
    def _():
        y_copy(0, False).wait_recv()

    @pl.when(has_low_x)
    def _():
        face_copy.wait_send()

    @pl.when(has_low_y)
    def _():
        y_copy(0, False).wait_send()

    row_start(coef_all, csend, crecv)
    wxu = jnp.concatenate([bx[1:], bx_in[...][None]], 0)
    wyu = jnp.where(row_y == size_y - 1, hy[0, 1], pltpu.roll(by, size_y - 1, 2))
    l0[WXU] = wxu
    l0[WYU] = wyu
    diagonal = alpha + bx + wxu + by + wyu + bz + wzu
    l0[DIAG] = diagonal
    inverse = 1.0 / diagonal
    l0[INV] = inverse

    def beside0(slot):
        field = v0[...]
        below_x = jnp.concatenate([hx[0][None], field[:-1]], 0)
        above_x = jnp.concatenate([field[1:], hx[1][None]], 0)
        below_y = jnp.where(row_y == 0, hy[slot, 0], pltpu.roll(field, 1, 2))
        above_y = jnp.where(row_y == size_y - 1, hy[slot, 1], pltpu.roll(field, size_y - 1, 2))
        total = l0[WXL] * below_x + l0[WXU] * above_x
        total = total + (l0[WYL] * below_y + l0[WYU] * above_y)
        return total + (l0[WZL] * z_lower(field) + l0[WZU] * z_upper(field))

    def publish(slot, colour, field):
        v0[...] = field
        ys[slot, 0] = field[:, :, size_y - 1 :]
        ys[slot, 1] = field[:, :, 0:1]
        start_exchange(slot, colour)

    publish(1, 0, jnp.where(red0, rhs * inverse, 0.0))
    for half in range(1, 2 * SWEEPS):
        slot = half % 2
        end_exchange(slot, (half - 1) % 2)
        updated = (l0[RHS] + beside0(slot)) * l0[INV]
        mask = red0 if half % 2 == 0 else jnp.logical_not(red0)
        if half >= 2:
            free_slot(1 - slot)
        publish(1 - slot, half % 2, jnp.where(mask, updated, v0[...]))
        if half == 2:
            row_wait(coef_all, csend, crecv)
            column_start(coef_all, csend, crecv)
        if half == 5:
            column_wait(coef_all, csend, crecv)
            core_copy(coef_all, csend, crecv, core).start()
    end_exchange(0, 1)
    residual0 = l0[RHS] - (l0[DIAG] * v0[...] - beside0(0))
    put(src_all.at[column, gx], pair_z(pair_x(residual0)), True, 0.125)
    row_start(src_all, gsend, grecv)
    free_slot(1)
    free_slot(0)
    core_copy(coef_all, csend, crecv, 1 - core).wait_recv()
    core_copy(coef_all, csend, crecv, core).wait_send()

    size_p = own_p * ngy
    shape1 = (ngx, 2, 2, 2, size_p, quarter)
    S1, INV1, DIAG1, WYL1, WZL1, UPPER1 = range(6)

    def whole_field(ref, number, block):
        parts = []
        for j in range(ngy):
            k = j % 2 * chips + j // 2
            parts.append(ref[k, block] if number is None else ref[k, block, number])
        return jnp.concatenate(parts, 3)

    wx1[ngx] = jnp.zeros(shape1[1:], F32)
    v1[...] = jnp.zeros(v1.shape, F32)
    row_p = lax.broadcasted_iota(jnp.int32, shape1[2:], 2)
    lane1 = lax.broadcasted_iota(jnp.int32, shape1[2:], 3)
    half_r = lax.broadcasted_iota(jnp.int32, shape1[2:], 0)
    half_s = lax.broadcasted_iota(jnp.int32, shape1[2:], 1)

    def coefs(block, carry):
        wx1[block] = whole_field(coef_all, 1, block)
        return carry

    lax.fori_loop(0, ngx, coefs, 0)

    def more_coefs(block, carry):
        a1 = whole_field(coef_all, 0, block)
        lower_x = wx1[block]
        next_x = wx1[block + 1]
        upper_x = jnp.stack([lower_x[1], next_x[0]], 0)
        lower_y = whole_field(coef_all, 2, block)
        upper_y = jnp.stack([lower_y[:, :, 1], pltpu.roll(lower_y[:, :, 0], size_p - 1, 2)], 2)
        upper_y = jnp.where((half_s == 1) & (row_p == size_p - 1), 0.0, upper_y)
        lower_z = whole_field(coef_all, 3, block)
        upper_z = jnp.stack([lower_z[:, 1], pltpu.roll(lower_z[:, 0], quarter - 1, 3)], 1)
        upper_z = jnp.where((half_r == 1) & (lane1 == quarter - 1), 0.0, upper_z)
        diagonal1 = a1 + lower_x + upper_x + lower_y + upper_y + lower_z + upper_z
        l1[DIAG1, block] = diagonal1
        l1[INV1, block] = 1.0 / diagonal1
        l1[WYL1, block] = lower_y
        l1[UPPER1, block, :, 0] = upper_y[:, :, 1]
        l1[WZL1, block] = lower_z
        l1[UPPER1, block, :, 1] = upper_z[:, 1]
        return carry

    lax.fori_loop(0, ngx, more_coefs, 0)

    shape2 = (ngx, size_p, quarter)
    row2 = lax.broadcasted_iota(jnp.int32, shape2, 1)
    lane2 = lax.broadcasted_iota(jnp.int32, shape2, 2)
    block2 = lax.broadcasted_iota(jnp.int32, shape2, 0)
    red2 = (block2 + row2 + lane2) % 2 == 0

    def summed(ref, fixed):
        total = None
        for xl in (0, 1):
            for r in (0, 1):
                for s in (0, 1):
                    if (xl, r, s)[fixed] == 0:
                        term = ref(xl, r, s)
                        total = term if total is None else total + term
        return total

    a2_parts = None
    for j in range(ngy):
        k = j % 2 * chips + j // 2
        part = None
        for xl in (0, 1):
            for r in (0, 1):
                for s in (0, 1):
                    term = coef_all[k, :, 0, xl, r, s]
                    part = term if part is None else part + term
        a2_parts = [part] if a2_parts is None else a2_parts + [part]
    a2 = jnp.concatenate(a2_parts, 1) * 0.125
    lower_x2 = summed(lambda xl, r, s: wx1[0:ngx, xl, r, s], 0) * 0.0625
    lower_y2 = summed(lambda xl, r, s: l1[WYL1, :, xl, r, s], 2) * 0.0625
    lower_z2 = summed(lambda xl, r, s: l1[WZL1, :, xl, r, s], 1) * 0.0625
    upper_x2 = jnp.concatenate([lower_x2[1:], jnp.zeros((1, size_p, quarter), F32)], 0)
    upper_y2 = jnp.where(row2 == size_p - 1, 0.0, pltpu.roll(lower_y2, size_p - 1, 1))
    upper_z2 = jnp.where(lane2 == quarter - 1, 0.0, pltpu.roll(lower_z2, quarter - 1, 2))
    diagonal2 = a2 + lower_x2 + upper_x2 + lower_y2 + upper_y2 + lower_z2 + upper_z2
    A2, WXL2, WXU2, WYL2, WYU2, WZL2, WZU2 = range(7)
    c2[A2] = 1.0 / diagonal2
    c2[WXL2] = lower_x2
    c2[WXU2] = upper_x2
    c2[WYL2] = jnp.where(row2 == 0, 0.0, lower_y2)
    c2[WYU2] = upper_y2
    c2[WZL2] = jnp.where(lane2 == 0, 0.0, lower_z2)
    c2[WZU2] = upper_z2
    for xl in (0, 1):
        for r in (0, 1):
            l1[WYL1, :, xl, r, 0] = jnp.where(row2 == 0, 0.0, l1[WYL1, :, xl, r, 0])
        for s in (0, 1):
            l1[WZL1, :, xl, 0, s] = jnp.where(lane2 == 0, 0.0, l1[WZL1, :, xl, 0, s])

    row_wait(src_all, gsend, grecv)
    column_start(src_all, gsend, grecv)
    column_wait(src_all, gsend, grecv)
    core_copy(src_all, gsend, grecv, core).start()
    core_copy(src_all, gsend, grecv, 1 - core).wait_recv()

    for block in range(ngx):
        l1[S1, block] = whole_field(src_all, None, block)

    def beside1(xl, r, s):
        if xl == 0:
            below_x = v1[0:ngx, 1, r, s]
            above_x = v1[1 : ngx + 1, 1, r, s]
            face_above = wx1[0:ngx, 1, r, s]
        else:
            below_x = v1[1 : ngx + 1, 0, r, s]
            above_x = v1[2 : ngx + 2, 0, r, s]
            face_above = wx1[1 : ngx + 1, 0, r, s]
        side_y = v1[1 : ngx + 1, xl, r, 1 - s]
        side_z = v1[1 : ngx + 1, xl, 1 - r, s]
        below_y = pltpu.roll(side_y, 1, 1) if s == 0 else side_y
        above_y = side_y if s == 0 else pltpu.roll(side_y, size_p - 1, 1)
        below_z = pltpu.roll(side_z, 1, 2) if r == 0 else side_z
        above_z = side_z if r == 0 else pltpu.roll(side_z, quarter - 1, 2)
        total = wx1[0:ngx, xl, r, s] * below_x + face_above * above_x
        upper_y = l1[WYL1, :, xl, r, 1] if s == 0 else l1[UPPER1, :, xl, 0, r]
        upper_z = l1[WZL1, :, xl, 1, s] if r == 0 else l1[UPPER1, :, xl, 1, s]
        total = total + (l1[WYL1, :, xl, r, s] * below_y + upper_y * above_y)
        return total + (l1[WZL1, :, xl, r, s] * below_z + upper_z * above_z)

    def half1(colour):
        for xl in (0, 1):
            for r in (0, 1):
                s = (xl + r + colour) % 2
                v1[1 : ngx + 1, xl, r, s] = (
                    l1[S1, :, xl, r, s] + beside1(xl, r, s)
                ) * l1[INV1, :, xl, r, s]

    def sweep1(number, carry):
        half1(0)
        half1(1)
        return carry

    lax.fori_loop(0, SWEEPS, sweep1, 0)

    source2 = None
    for xl in (0, 1):
        for r in (0, 1):
            for s in (0, 1):
                term = l1[S1, :, xl, r, s] - (
                    l1[DIAG1, :, xl, r, s] * v1[1 : ngx + 1, xl, r, s] - beside1(xl, r, s)
                )
                source2 = term if source2 is None else source2 + term
    source2 = source2 * 0.125

    zero_block = jnp.zeros((1, size_p, quarter), F32)

    def half2(field, mask):
        below_x = jnp.concatenate([zero_block, field[:-1]], 0)
        above_x = jnp.concatenate([field[1:], zero_block], 0)
        total = c2[WXL2] * below_x + c2[WXU2] * above_x
        total = total + (
            c2[WYL2] * pltpu.roll(field, 1, 1) + c2[WYU2] * pltpu.roll(field, size_p - 1, 1)
        )
        total = total + (
            c2[WZL2] * pltpu.roll(field, 1, 2) + c2[WZU2] * pltpu.roll(field, quarter - 1, 2)
        )
        return jnp.where(mask, (source2 + total) * c2[A2], field)

    def sweep2(number, field):
        return half2(half2(field, red2), jnp.logical_not(red2))

    core_copy(src_all, gsend, grecv, core).wait_send()
    coarse = lax.fori_loop(0, COARSE_SWEEPS, sweep2, jnp.zeros(shape2, F32))
    c2[A2] = coarse

    shift = lax.rem(size_p - own_p * gy, size_p)
    own_coarse = c2[A2, gx]
    coarse_ref[0] = pltpu.roll(own_coarse, shift, 0)[:own_p]
    for xl in (0, 1):
        for r in (0, 1):
            for s in (0, 1):
                tile = pltpu.roll(v1[gx + 1, xl, r, s] + own_coarse, shift, 0)[:own_p]
                spread[xl, r, pl.ds(2 * s, own_p, stride=4), :] = tile
                spread[xl, r, pl.ds(2 * s + 1, own_p, stride=4), :] = tile
    added = []
    for x in range(size_x):
        added.append(jnp.concatenate([v0[x, r] + spread[x // 2, r // 2] for r in range(4)], 1))
    natural = permuted(jnp.concatenate(added, 0), order_matrix(size_z, True))
    fine_ref[...] = natural.reshape(size_x, size_y, size_z)


def on_device(ngx, ngy, rhs, alpha, beta_x, beta_y, beta_z):
    size_x, size_y, size_z = rhs.shape
    quarter = size_z // 4
    own_p = size_y // 4
    size_p = own_p * ngy
    field0 = (size_x, 4, size_y, quarter)
    block1 = (2, 2, 2, size_p, quarter)
    piece1 = (2, 2, 2, own_p, quarter)
    dma = pltpu.SemaphoreType.DMA
    most = max(ngx, ngy)
    return pl.pallas_call(
        functools.partial(kernel, ngx, ngy),
        out_shape=(
            jax.ShapeDtypeStruct(rhs.shape, F32),
            jax.ShapeDtypeStruct((size_x // 4, own_p, quarter), F32),
        ),
        in_specs=[pl.BlockSpec(memory_space=pltpu.VMEM)] * 5,
        out_specs=(pl.BlockSpec(memory_space=pltpu.VMEM),) * 2,
        scratch_shapes=[
            pltpu.VMEM((9,) + field0, F32),
            pltpu.VMEM(field0, F32),
            pltpu.VMEM((2,) + field0[1:], F32),
            pltpu.VMEM(field0[1:], F32),
            pltpu.VMEM((2, 2, 4, size_y // 2, quarter), F32),
            pltpu.VMEM((2, 2, 4, size_y // 2, quarter), F32),
            pltpu.VMEM((2, 2, size_x, 4, 1, quarter), F32),
            pltpu.VMEM((2, 2, size_x, 4, 1, quarter), F32),
            pltpu.VMEM((size_x // 2, 2, size_y, quarter), F32),
            pltpu.VMEM((ngy, ngx) + piece1, F32),
            pltpu.VMEM((ngy, ngx, 4) + piece1, F32),
            pltpu.VMEM((6, ngx) + block1, F32),
            pltpu.VMEM((ngx + 1,) + block1, F32),
            pltpu.VMEM((ngx + 2,) + block1, F32),
            pltpu.VMEM((7, ngx, size_p, quarter), F32),
            pltpu.VMEM((2, 2, size_y, quarter), F32),
            dma((3, 2)), dma((3, 2)), dma((2, 2)), dma((2, 2)),
            dma((3, most)), dma((3, most)), dma((3, most)), dma((3, most)),
        ],
        compiler_params=pltpu.CompilerParams(
            collective_id=0, has_side_effects=True, vmem_limit_bytes=62 * 1024 * 1024
        ),
    )(rhs, alpha, beta_x, beta_y, beta_z)


def solution(mesh):
    spec = P("gx", "gy", None)
    return jax.shard_map(
        functools.partial(on_device, mesh.shape["gx"], mesh.shape["gy"]),
        mesh=mesh,
        in_specs=(spec,) * 5,
        out_specs=(spec, spec),
        check_vma=False,
    )
```

```python
import functools

import jax
import jax.numpy as jnp
from jax import lax
from jax.experimental import pallas as pl
from jax.experimental.pallas import tpu as pltpu
from jax.sharding import PartitionSpec as P

SWEEPS = 4
COARSE_SWEEPS = 8
MESH = pl.DeviceIdType.MESH
F32 = jnp.float32
LANES = 128


def order_matrix(size):
    quarter = size // 4
    row = lax.broadcasted_iota(jnp.int32, (size, quarter), 0)
    col = lax.broadcasted_iota(jnp.int32, (size, quarter), 1)
    difference = row - 4 * col
    return jnp.concatenate(
        [jnp.where(difference == r, 1.0, 0.0).astype(jnp.bfloat16) for r in range(4)], 1
    )


def permuted(rows, matrix, back):
    count = rows.shape[0]
    high = rows.astype(jnp.bfloat16)
    rest = rows - high.astype(F32)
    middle = rest.astype(jnp.bfloat16)
    low = (rest - middle.astype(F32)).astype(jnp.bfloat16)
    stacked = jnp.concatenate([high, middle, low], 0)
    out = lax.dot_general(
        stacked, matrix, (((1,), (1 if back else 0,)), ((), ())), preferred_element_type=F32
    )
    return (out[2 * count :] + out[count : 2 * count]) + out[:count]


def kernel(
    ngx, ngy,
    rhs_ref, alpha_ref, bx_ref, by_ref, bz_ref,
    fine_ref, coarse_ref,
    l0, v0, hx, bx_in, px, qx, ys, hy, pairs, src_all, coef_all, l1, wx1, v1, c2, spread, order,
    xsend, xrecv, ysend, yrecv, gsend, grecv, csend, crecv,
):
    gx = lax.axis_index("gx")
    gy = lax.axis_index("gy")
    size_x, size_y, size_z = rhs_ref.shape
    quarter = size_z // 4
    own_p = size_y // 4
    chips, chip, core = ngy // 2, gy // 2, lax.rem(gy, 2)
    column = core * chips + chip
    shape0 = (size_x, 4, size_y, quarter)

    hx[...] = jnp.zeros(hx.shape, F32)
    bx_in[...] = jnp.zeros(bx_in.shape, F32)
    hy[...] = jnp.zeros(hy.shape, F32)

    barrier = pltpu.get_barrier_semaphore()

    def greet_x(step, carry):
        other = lax.rem(gx + step, ngx)
        pl.semaphore_signal(barrier, inc=1, device_id=(other, gy), device_id_type=MESH)
        return carry

    def greet_y(step, carry):
        other = lax.rem(gy + step, ngy)
        pl.semaphore_signal(barrier, inc=1, device_id=(gx, other), device_id_type=MESH)
        return carry

    lax.fori_loop(1, ngx, greet_x, 0)
    lax.fori_loop(1, ngy, greet_y, 0)

    matrix = order_matrix(size_z)
    order[...] = matrix
    rows = size_x * size_y
    stacked = jnp.concatenate(
        [ref[...].reshape(rows, size_z) for ref in (rhs_ref, alpha_ref, bx_ref, by_ref, bz_ref)], 0
    )
    ordered = permuted(stacked, matrix, False)

    def ordered_field(number):
        whole = ordered[number * rows : (number + 1) * rows].reshape(size_x, size_y, size_z)
        return jnp.stack([whole[:, :, r * quarter : (r + 1) * quarter] for r in range(4)], 1)

    rhs, alpha, bx, by, bz = [ordered_field(number) for number in range(5)]
    RHS, INV, DIAG, WXL, WXU, WYL, WYU, WZL, WZU = range(9)
    l0[RHS] = rhs
    l0[WXL] = bx
    l0[WYL] = by

    pl.semaphore_wait(barrier, ngx - 1 + ngy - 1)

    def x_copy(slot, up):
        side = 0 if up else 1
        return pltpu.make_async_remote_copy(
            src_ref=px.at[slot, side],
            dst_ref=qx.at[slot, side],
            send_sem=xsend.at[slot, side],
            recv_sem=xrecv.at[slot, side],
            device_id=(gx + 1 if up else gx - 1, gy),
            device_id_type=MESH,
        )

    def y_copy(slot, up):
        side = 0 if up else 1
        return pltpu.make_async_remote_copy(
            src_ref=ys.at[slot, side],
            dst_ref=hy.at[slot, side],
            send_sem=ysend.at[slot, side],
            recv_sem=yrecv.at[slot, side],
            device_id=(gx, gy + 1 if up else gy - 1),
            device_id_type=MESH,
        )

    face_copy = pltpu.make_async_remote_copy(
        src_ref=l0.at[WXL, 0],
        dst_ref=bx_in,
        send_sem=xsend.at[2, 0],
        recv_sem=xrecv.at[2, 0],
        device_id=(gx - 1, gy),
        device_id_type=MESH,
    )

    has_low_x, has_high_x = gx > 0, gx < ngx - 1
    has_low_y, has_high_y = gy > 0, gy < ngy - 1

    def strided(colour, up, r):
        x = size_x - 1 if up else 0
        return pl.ds((colour + x + r) % 2, size_y // 2, stride=2)

    def start_exchange(slot, colour):
        for up in (False, True):
            side = 0 if up else 1
            plane = size_x - 1 if up else 0

            @pl.when(has_high_x if up else has_low_x)
            def _():
                for r in range(4):
                    px[slot, side, r] = v0[plane, r, strided(colour, up, r), :]
                x_copy(slot, up).start()
        for up in (False, True):
            @pl.when(has_high_y if up else has_low_y)
            def _():
                y_copy(slot, up).start()

    def end_exchange(slot, colour):
        for up in (False, True):
            side = 0 if up else 1

            @pl.when(has_low_y if up else has_high_y)
            def _():
                y_copy(slot, up).wait_recv()

            @pl.when(has_low_x if up else has_high_x)
            def _():
                x_copy(slot, up).wait_recv()
                for r in range(4):
                    hx[side, r, strided(colour, up, r), :] = qx[slot, side, r]

    def free_slot(slot):
        for up in (False, True):
            @pl.when(has_high_x if up else has_low_x)
            def _():
                x_copy(slot, up).wait_send()

            @pl.when(has_high_y if up else has_low_y)
            def _():
                y_copy(slot, up).wait_send()

    ys[0, 1] = by[:, :, 0:1]

    @pl.when(has_low_x)
    def _():
        face_copy.start()

    @pl.when(has_low_y)
    def _():
        y_copy(0, False).start()

    def pair_x(field):
        grouped = field.reshape(size_x // 2, 2, *field.shape[1:])
        return grouped[:, 0] + grouped[:, 1]

    def first_x(field):
        return field.reshape(size_x // 2, 2, *field.shape[1:])[:, 0]

    def pair_z(field):
        return jnp.stack([field[:, 0] + field[:, 1], field[:, 2] + field[:, 3]], 1)

    def first_z(field):
        return jnp.stack([field[:, 0], field[:, 2]], 1)

    def packed(field, pair_y):
        if pair_y:
            field = field + pltpu.roll(field, size_y - 1, 2)
        pairs[...] = field
        even = pairs[:, :, pl.ds(0, own_p, stride=4), :]
        odd = pairs[:, :, pl.ds(2, own_p, stride=4), :]
        return even, odd

    def put(ref, field, pair_y, scale):
        even, odd = packed(field * scale, pair_y)
        ref[:, :, 0] = even
        ref[:, :, 1] = odd

    put(coef_all.at[column, gx, 0], pair_z(pair_x(alpha)), True, 0.125)
    put(coef_all.at[column, gx, 1], pair_z(first_x(bx)), True, 0.0625)
    put(coef_all.at[column, gx, 2], pair_z(pair_x(by)), False, 0.0625)
    put(coef_all.at[column, gx, 3], first_z(pair_x(bz)), True, 0.0625)

    def row_copy(ref, ssem, rsem, other, slot):
        return pltpu.make_async_remote_copy(
            src_ref=ref.at[column, gx], dst_ref=ref.at[column, slot],
            send_sem=ssem.at[0, other], recv_sem=rsem.at[0, slot],
            device_id=(other, gy), device_id_type=MESH,
        )

    def column_copy(ref, ssem, rsem, other, slot):
        return pltpu.make_async_remote_copy(
            src_ref=ref.at[column], dst_ref=ref.at[core * chips + slot],
            send_sem=ssem.at[1, other], recv_sem=rsem.at[1, slot],
            device_id=(gx, 2 * other + core), device_id_type=MESH,
        )

    def core_copy(ref, ssem, rsem, slot):
        whole = ref.at[pl.ds(slot * chips, chips)]
        return pltpu.make_async_remote_copy(
            src_ref=whole, dst_ref=whole,
            send_sem=ssem.at[2, 0], recv_sem=rsem.at[2, 0],
            device_id=(gx, 2 * chip + 1 - core), device_id_type=MESH,
        )

    def each_other(count, me, action):
        def step(number, carry):
            action(lax.rem(me + number, count))
            return carry

        lax.fori_loop(1, count, step, 0)

    def row_start(ref, ssem, rsem):
        each_other(ngx, gx, lambda other: row_copy(ref, ssem, rsem, other, gx).start())

    def row_wait(ref, ssem, rsem):
        each_other(ngx, gx, lambda other: row_copy(ref, ssem, rsem, other, other).wait_recv())
        each_other(ngx, gx, lambda other: row_copy(ref, ssem, rsem, other, gx).wait_send())

    def column_start(ref, ssem, rsem):
        each_other(chips, chip, lambda other: column_copy(ref, ssem, rsem, other, chip).start())

    def column_wait(ref, ssem, rsem):
        each_other(chips, chip, lambda other: column_copy(ref, ssem, rsem, other, other).wait_recv())
        each_other(chips, chip, lambda other: column_copy(ref, ssem, rsem, other, chip).wait_send())

    row_y = lax.broadcasted_iota(jnp.int32, shape0, 2)
    lane = lax.broadcasted_iota(jnp.int32, shape0, 3)
    residue = lax.broadcasted_iota(jnp.int32, shape0, 1)
    row_x = lax.broadcasted_iota(jnp.int32, shape0, 0)
    offset = gx * size_x + gy * size_y
    red0 = ((row_x + residue + row_y + offset) & 1) == 0

    def z_lower(field):
        return jnp.concatenate([pltpu.roll(field[:, 3:], 1, 3), field[:, :3]], 1)

    def z_upper(field):
        return jnp.concatenate([field[:, 1:], pltpu.roll(field[:, :1], quarter - 1, 3)], 1)

    wzu = jnp.where((residue == 3) & (lane == quarter - 1), 0.0, z_upper(bz))
    l0[WZU] = wzu
    l0[WZL] = jnp.where((residue == 0) & (lane == 0), 0.0, bz)

    @pl.when(has_high_x)
    def _():
        face_copy.wait_recv()

    @pl.when(has_high_y)
    def _():
        y_copy(0, False).wait_recv()

    @pl.when(has_low_x)
    def _():
        face_copy.wait_send()

    @pl.when(has_low_y)
    def _():
        y_copy(0, False).wait_send()

    row_start(coef_all, csend, crecv)
    wxu = jnp.concatenate([bx[1:], bx_in[...][None]], 0)
    wyu = jnp.where(row_y == size_y - 1, hy[0, 1], pltpu.roll(by, size_y - 1, 2))
    l0[WXU] = wxu
    l0[WYU] = wyu
    diagonal = alpha + bx + wxu + by + wyu + bz + wzu
    l0[DIAG] = diagonal
    inverse = 1.0 / diagonal
    l0[INV] = inverse

    def beside0(slot):
        field = v0[...]
        below_x = jnp.concatenate([hx[0][None], field[:-1]], 0)
        above_x = jnp.concatenate([field[1:], hx[1][None]], 0)
        below_y = jnp.where(row_y == 0, hy[slot, 0], pltpu.roll(field, 1, 2))
        above_y = jnp.where(row_y == size_y - 1, hy[slot, 1], pltpu.roll(field, size_y - 1, 2))
        total = l0[WXL] * below_x + l0[WXU] * above_x
        total = total + (l0[WYL] * below_y + l0[WYU] * above_y)
        return total + (l0[WZL] * z_lower(field) + l0[WZU] * z_upper(field))

    def publish(slot, colour, field):
        v0[...] = field
        ys[slot, 0] = field[:, :, size_y - 1 :]
        ys[slot, 1] = field[:, :, 0:1]
        start_exchange(slot, colour)

    publish(1, 0, jnp.where(red0, rhs * inverse, 0.0))
    for half in range(1, 2 * SWEEPS):
        slot = half % 2
        end_exchange(slot, (half - 1) % 2)
        updated = (l0[RHS] + beside0(slot)) * l0[INV]
        mask = red0 if half % 2 == 0 else jnp.logical_not(red0)
        if half >= 2:
            free_slot(1 - slot)
        publish(1 - slot, half % 2, jnp.where(mask, updated, v0[...]))
        if half == 2:
            row_wait(coef_all, csend, crecv)
            column_start(coef_all, csend, crecv)
        if half == 5:
            column_wait(coef_all, csend, crecv)
            core_copy(coef_all, csend, crecv, core).start()
    end_exchange(0, 1)
    residual0 = l0[RHS] - (l0[DIAG] * v0[...] - beside0(0))
    put(src_all.at[column, gx], pair_z(pair_x(residual0)), True, 0.125)
    row_start(src_all, gsend, grecv)
    free_slot(1)
    free_slot(0)
    core_copy(coef_all, csend, crecv, 1 - core).wait_recv()
    core_copy(coef_all, csend, crecv, core).wait_send()

    size_p = own_p * ngy
    shape1 = (ngx, 2, 2, 2, size_p, quarter)
    S1, INV1, DIAG1, WYL1, WZL1, UPPER1 = range(6)

    def whole_field(ref, number, block):
        parts = []
        for j in range(ngy):
            k = j % 2 * chips + j // 2
            parts.append(ref[k, block] if number is None else ref[k, block, number])
        return jnp.concatenate(parts, 3)

    wx1[ngx] = jnp.zeros(shape1[1:], F32)
    v1[...] = jnp.zeros(v1.shape, F32)
    row_p = lax.broadcasted_iota(jnp.int32, shape1[2:], 2)
    lane1 = lax.broadcasted_iota(jnp.int32, shape1[2:], 3)
    half_r = lax.broadcasted_iota(jnp.int32, shape1[2:], 0)
    half_s = lax.broadcasted_iota(jnp.int32, shape1[2:], 1)

    def coefs(block, carry):
        wx1[block] = whole_field(coef_all, 1, block)
        return carry

    lax.fori_loop(0, ngx, coefs, 0)

    def more_coefs(block, carry):
        a1 = whole_field(coef_all, 0, block)
        lower_x = wx1[block]
        next_x = wx1[block + 1]
        upper_x = jnp.stack([lower_x[1], next_x[0]], 0)
        lower_y = whole_field(coef_all, 2, block)
        upper_y = jnp.stack([lower_y[:, :, 1], pltpu.roll(lower_y[:, :, 0], size_p - 1, 2)], 2)
        upper_y = jnp.where((half_s == 1) & (row_p == size_p - 1), 0.0, upper_y)
        lower_z = whole_field(coef_all, 3, block)
        upper_z = jnp.stack([lower_z[:, 1], pltpu.roll(lower_z[:, 0], quarter - 1, 3)], 1)
        upper_z = jnp.where((half_r == 1) & (lane1 == quarter - 1), 0.0, upper_z)
        diagonal1 = a1 + lower_x + upper_x + lower_y + upper_y + lower_z + upper_z
        l1[DIAG1, block] = diagonal1
        l1[INV1, block] = 1.0 / diagonal1
        l1[WYL1, block] = lower_y
        l1[UPPER1, block, :, 0] = upper_y[:, :, 1]
        l1[WZL1, block] = lower_z
        l1[UPPER1, block, :, 1] = upper_z[:, 1]
        return carry

    lax.fori_loop(0, ngx, more_coefs, 0)

    shape2 = (ngx, size_p, quarter)
    row2 = lax.broadcasted_iota(jnp.int32, shape2, 1)
    lane2 = lax.broadcasted_iota(jnp.int32, shape2, 2)
    block2 = lax.broadcasted_iota(jnp.int32, shape2, 0)
    red2 = ((block2 + row2 + lane2) & 1) == 0

    def summed(ref, fixed):
        total = None
        for xl in (0, 1):
            for r in (0, 1):
                for s in (0, 1):
                    if (xl, r, s)[fixed] == 0:
                        term = ref(xl, r, s)
                        total = term if total is None else total + term
        return total

    a2_parts = None
    for j in range(ngy):
        k = j % 2 * chips + j // 2
        part = None
        for xl in (0, 1):
            for r in (0, 1):
                for s in (0, 1):
                    term = coef_all[k, :, 0, xl, r, s]
                    part = term if part is None else part + term
        a2_parts = [part] if a2_parts is None else a2_parts + [part]
    a2 = jnp.concatenate(a2_parts, 1) * 0.125
    lower_x2 = summed(lambda xl, r, s: wx1[0:ngx, xl, r, s], 0) * 0.0625
    lower_y2 = summed(lambda xl, r, s: l1[WYL1, :, xl, r, s], 2) * 0.0625
    lower_z2 = summed(lambda xl, r, s: l1[WZL1, :, xl, r, s], 1) * 0.0625
    upper_x2 = jnp.concatenate([lower_x2[1:], jnp.zeros((1, size_p, quarter), F32)], 0)
    upper_y2 = jnp.where(row2 == size_p - 1, 0.0, pltpu.roll(lower_y2, size_p - 1, 1))
    upper_z2 = jnp.where(lane2 == quarter - 1, 0.0, pltpu.roll(lower_z2, quarter - 1, 2))
    diagonal2 = a2 + lower_x2 + upper_x2 + lower_y2 + upper_y2 + lower_z2 + upper_z2
    A2, WXL2, WXU2, WYL2, WYU2, WZL2, WZU2 = range(7)
    c2[A2] = 1.0 / diagonal2
    c2[WXL2] = lower_x2
    c2[WXU2] = upper_x2
    c2[WYL2] = jnp.where(row2 == 0, 0.0, lower_y2)
    c2[WYU2] = upper_y2
    c2[WZL2] = jnp.where(lane2 == 0, 0.0, lower_z2)
    c2[WZU2] = upper_z2
    for xl in (0, 1):
        for r in (0, 1):
            l1[WYL1, :, xl, r, 0] = jnp.where(row2 == 0, 0.0, l1[WYL1, :, xl, r, 0])
        for s in (0, 1):
            l1[WZL1, :, xl, 0, s] = jnp.where(lane2 == 0, 0.0, l1[WZL1, :, xl, 0, s])

    row_wait(src_all, gsend, grecv)
    column_start(src_all, gsend, grecv)
    column_wait(src_all, gsend, grecv)
    core_copy(src_all, gsend, grecv, core).start()
    core_copy(src_all, gsend, grecv, 1 - core).wait_recv()

    for block in range(ngx):
        l1[S1, block] = whole_field(src_all, None, block)

    def beside1(xl, r, s):
        if xl == 0:
            below_x = v1[0:ngx, 1, r, s]
            above_x = v1[1 : ngx + 1, 1, r, s]
            face_above = wx1[0:ngx, 1, r, s]
        else:
            below_x = v1[1 : ngx + 1, 0, r, s]
            above_x = v1[2 : ngx + 2, 0, r, s]
            face_above = wx1[1 : ngx + 1, 0, r, s]
        side_y = v1[1 : ngx + 1, xl, r, 1 - s]
        side_z = v1[1 : ngx + 1, xl, 1 - r, s]
        below_y = pltpu.roll(side_y, 1, 1) if s == 0 else side_y
        above_y = side_y if s == 0 else pltpu.roll(side_y, size_p - 1, 1)
        below_z = pltpu.roll(side_z, 1, 2) if r == 0 else side_z
        above_z = side_z if r == 0 else pltpu.roll(side_z, quarter - 1, 2)
        total = wx1[0:ngx, xl, r, s] * below_x + face_above * above_x
        upper_y = l1[WYL1, :, xl, r, 1] if s == 0 else l1[UPPER1, :, xl, 0, r]
        upper_z = l1[WZL1, :, xl, 1, s] if r == 0 else l1[UPPER1, :, xl, 1, s]
        total = total + (l1[WYL1, :, xl, r, s] * below_y + upper_y * above_y)
        return total + (l1[WZL1, :, xl, r, s] * below_z + upper_z * above_z)

    def half1(colour):
        for xl in (0, 1):
            for r in (0, 1):
                s = (xl + r + colour) % 2
                v1[1 : ngx + 1, xl, r, s] = (
                    l1[S1, :, xl, r, s] + beside1(xl, r, s)
                ) * l1[INV1, :, xl, r, s]

    def sweep1(number, carry):
        half1(0)
        half1(1)
        return carry

    lax.fori_loop(0, SWEEPS, sweep1, 0)

    source2 = None
    for xl in (0, 1):
        for r in (0, 1):
            for s in (0, 1):
                term = l1[S1, :, xl, r, s] - (
                    l1[DIAG1, :, xl, r, s] * v1[1 : ngx + 1, xl, r, s] - beside1(xl, r, s)
                )
                source2 = term if source2 is None else source2 + term
    source2 = source2 * 0.125

    zero_block = jnp.zeros((1, size_p, quarter), F32)

    def half2(field, mask):
        below_x = jnp.concatenate([zero_block, field[:-1]], 0)
        above_x = jnp.concatenate([field[1:], zero_block], 0)
        total = c2[WXL2] * below_x + c2[WXU2] * above_x
        total = total + (
            c2[WYL2] * pltpu.roll(field, 1, 1) + c2[WYU2] * pltpu.roll(field, size_p - 1, 1)
        )
        total = total + (
            c2[WZL2] * pltpu.roll(field, 1, 2) + c2[WZU2] * pltpu.roll(field, quarter - 1, 2)
        )
        return jnp.where(mask, (source2 + total) * c2[A2], field)

    def sweep2(number, field):
        return half2(half2(field, red2), jnp.logical_not(red2))

    core_copy(src_all, gsend, grecv, core).wait_send()
    coarse = lax.fori_loop(0, COARSE_SWEEPS, sweep2, jnp.zeros(shape2, F32))
    c2[A2] = coarse

    shift = lax.rem(size_p - own_p * gy, size_p)
    own_coarse = c2[A2, gx]
    coarse_ref[0] = pltpu.roll(own_coarse, shift, 0)[:own_p]
    for xl in (0, 1):
        for r in (0, 1):
            for s in (0, 1):
                tile = pltpu.roll(v1[gx + 1, xl, r, s] + own_coarse, shift, 0)[:own_p]
                spread[xl, r, pl.ds(2 * s, own_p, stride=4), :] = tile
                spread[xl, r, pl.ds(2 * s + 1, own_p, stride=4), :] = tile
    added = []
    for x in range(size_x):
        added.append(jnp.concatenate([v0[x, r] + spread[x // 2, r // 2] for r in range(4)], 1))
    natural = permuted(jnp.concatenate(added, 0), order[...], True)
    fine_ref[...] = natural.reshape(size_x, size_y, size_z)


def on_device(ngx, ngy, rhs, alpha, beta_x, beta_y, beta_z):
    size_x, size_y, size_z = rhs.shape
    quarter = size_z // 4
    own_p = size_y // 4
    size_p = own_p * ngy
    field0 = (size_x, 4, size_y, quarter)
    block1 = (2, 2, 2, size_p, quarter)
    piece1 = (2, 2, 2, own_p, quarter)
    dma = pltpu.SemaphoreType.DMA
    most = max(ngx, ngy)
    return pl.pallas_call(
        functools.partial(kernel, ngx, ngy),
        out_shape=(
            jax.ShapeDtypeStruct(rhs.shape, F32),
            jax.ShapeDtypeStruct((size_x // 4, own_p, quarter), F32),
        ),
        in_specs=[pl.BlockSpec(memory_space=pltpu.VMEM)] * 5,
        out_specs=(pl.BlockSpec(memory_space=pltpu.VMEM),) * 2,
        scratch_shapes=[
            pltpu.VMEM((9,) + field0, F32),
            pltpu.VMEM(field0, F32),
            pltpu.VMEM((2,) + field0[1:], F32),
            pltpu.VMEM(field0[1:], F32),
            pltpu.VMEM((2, 2, 4, size_y // 2, quarter), F32),
            pltpu.VMEM((2, 2, 4, size_y // 2, quarter), F32),
            pltpu.VMEM((2, 2, size_x, 4, 1, quarter), F32),
            pltpu.VMEM((2, 2, size_x, 4, 1, quarter), F32),
            pltpu.VMEM((size_x // 2, 2, size_y, quarter), F32),
            pltpu.VMEM((ngy, ngx) + piece1, F32),
            pltpu.VMEM((ngy, ngx, 4) + piece1, F32),
            pltpu.VMEM((6, ngx) + block1, F32),
            pltpu.VMEM((ngx + 1,) + block1, F32),
            pltpu.VMEM((ngx + 2,) + block1, F32),
            pltpu.VMEM((7, ngx, size_p, quarter), F32),
            pltpu.VMEM((2, 2, size_y, quarter), F32),
            pltpu.VMEM((size_z, size_z), jnp.bfloat16),
            dma((3, 2)), dma((3, 2)), dma((2, 2)), dma((2, 2)),
            dma((3, most)), dma((3, most)), dma((3, most)), dma((3, most)),
        ],
        compiler_params=pltpu.CompilerParams(
            collective_id=0, has_side_effects=True, vmem_limit_bytes=62 * 1024 * 1024
        ),
    )(rhs, alpha, beta_x, beta_y, beta_z)


def solution(mesh):
    spec = P("gx", "gy", None)
    return jax.shard_map(
        functools.partial(on_device, mesh.shape["gx"], mesh.shape["gy"]),
        mesh=mesh,
        in_specs=(spec,) * 5,
        out_specs=(spec, spec),
        check_vma=False,
    )
```

```python
import functools

import jax
import jax.numpy as jnp
from jax import lax
from jax.experimental import pallas as pl
from jax.experimental.pallas import tpu as pltpu
from jax.sharding import PartitionSpec as P

SWEEPS = 4
COARSE_SWEEPS = 8
MESH = pl.DeviceIdType.MESH
F32 = jnp.float32
LANES = 128


def order_matrix(size):
    quarter = size // 4
    row = lax.broadcasted_iota(jnp.int32, (size, quarter), 0)
    col = lax.broadcasted_iota(jnp.int32, (size, quarter), 1)
    difference = row - 4 * col
    return jnp.concatenate(
        [jnp.where(difference == r, 1.0, 0.0).astype(jnp.bfloat16) for r in range(4)], 1
    )


def permuted(rows, matrix, back):
    count = rows.shape[0]
    high = rows.astype(jnp.bfloat16)
    rest = rows - high.astype(F32)
    middle = rest.astype(jnp.bfloat16)
    low = (rest - middle.astype(F32)).astype(jnp.bfloat16)
    stacked = jnp.concatenate([high, middle, low], 0)
    out = lax.dot_general(
        stacked, matrix, (((1,), (1 if back else 0,)), ((), ())), preferred_element_type=F32
    )
    return (out[2 * count :] + out[count : 2 * count]) + out[:count]


def kernel(
    ngx, ngy,
    rhs_ref, alpha_ref, bx_ref, by_ref, bz_ref,
    fine_ref, coarse_ref,
    l0, v0, hx, bx_in, px, qx, ys, hy, pairs, src_all, coef_all, l1, wx1, v1, c2, spread, order,
    xsend, xrecv, ysend, yrecv, gsend, grecv, csend, crecv,
):
    gx = lax.axis_index("gx")
    gy = lax.axis_index("gy")
    size_x, size_y, size_z = rhs_ref.shape
    quarter = size_z // 4
    own_p = size_y // 4
    chips, chip, core = ngy // 2, gy // 2, lax.rem(gy, 2)
    column = core * chips + chip
    pairs_x, pos_x, side_x = ngx // 2, gx // 2, lax.rem(gx, 2)
    place = side_x * pairs_x + pos_x
    shape0 = (size_x, 4, size_y, quarter)

    hx[...] = jnp.zeros(hx.shape, F32)
    bx_in[...] = jnp.zeros(bx_in.shape, F32)
    hy[...] = jnp.zeros(hy.shape, F32)

    barrier = pltpu.get_barrier_semaphore()

    def greet_x(step, carry):
        other = lax.rem(gx + step, ngx)
        pl.semaphore_signal(barrier, inc=1, device_id=(other, gy), device_id_type=MESH)
        return carry

    def greet_y(step, carry):
        other = lax.rem(gy + step, ngy)
        pl.semaphore_signal(barrier, inc=1, device_id=(gx, other), device_id_type=MESH)
        return carry

    lax.fori_loop(1, ngx, greet_x, 0)
    lax.fori_loop(1, ngy, greet_y, 0)

    matrix = order_matrix(size_z)
    order[...] = matrix
    rows = size_x * size_y
    stacked = jnp.concatenate(
        [ref[...].reshape(rows, size_z) for ref in (rhs_ref, alpha_ref, bx_ref, by_ref, bz_ref)], 0
    )
    ordered = permuted(stacked, matrix, False)

    def ordered_field(number):
        whole = ordered[number * rows : (number + 1) * rows].reshape(size_x, size_y, size_z)
        return jnp.stack([whole[:, :, r * quarter : (r + 1) * quarter] for r in range(4)], 1)

    rhs, alpha, bx, by, bz = [ordered_field(number) for number in range(5)]
    RHS, INV, DIAG, WXL, WXU, WYL, WYU, WZL, WZU = range(9)
    l0[RHS] = rhs
    l0[WXL] = bx
    l0[WYL] = by

    pl.semaphore_wait(barrier, ngx - 1 + ngy - 1)

    def x_copy(slot, up):
        side = 0 if up else 1
        return pltpu.make_async_remote_copy(
            src_ref=px.at[slot, side],
            dst_ref=qx.at[slot, side],
            send_sem=xsend.at[slot, side],
            recv_sem=xrecv.at[slot, side],
            device_id=(gx + 1 if up else gx - 1, gy),
            device_id_type=MESH,
        )

    def y_copy(slot, up):
        side = 0 if up else 1
        return pltpu.make_async_remote_copy(
            src_ref=ys.at[slot, side],
            dst_ref=hy.at[slot, side],
            send_sem=ysend.at[slot, side],
            recv_sem=yrecv.at[slot, side],
            device_id=(gx, gy + 1 if up else gy - 1),
            device_id_type=MESH,
        )

    face_copy = pltpu.make_async_remote_copy(
        src_ref=l0.at[WXL, 0],
        dst_ref=bx_in,
        send_sem=xsend.at[2, 0],
        recv_sem=xrecv.at[2, 0],
        device_id=(gx - 1, gy),
        device_id_type=MESH,
    )

    has_low_x, has_high_x = gx > 0, gx < ngx - 1
    has_low_y, has_high_y = gy > 0, gy < ngy - 1

    def strided(colour, up, r):
        x = size_x - 1 if up else 0
        return pl.ds((colour + x + r) % 2, size_y // 2, stride=2)

    def start_exchange(slot, colour):
        for up in (False, True):
            side = 0 if up else 1
            plane = size_x - 1 if up else 0

            @pl.when(has_high_x if up else has_low_x)
            def _():
                for r in range(4):
                    px[slot, side, r] = v0[plane, r, strided(colour, up, r), :]
                x_copy(slot, up).start()
        for up in (False, True):
            @pl.when(has_high_y if up else has_low_y)
            def _():
                y_copy(slot, up).start()

    def end_exchange(slot, colour):
        for up in (False, True):
            side = 0 if up else 1

            @pl.when(has_low_y if up else has_high_y)
            def _():
                y_copy(slot, up).wait_recv()

            @pl.when(has_low_x if up else has_high_x)
            def _():
                x_copy(slot, up).wait_recv()
                for r in range(4):
                    hx[side, r, strided(colour, up, r), :] = qx[slot, side, r]

    def free_slot(slot):
        for up in (False, True):
            @pl.when(has_high_x if up else has_low_x)
            def _():
                x_copy(slot, up).wait_send()

            @pl.when(has_high_y if up else has_low_y)
            def _():
                y_copy(slot, up).wait_send()

    ys[0, 1] = by[:, :, 0:1]

    @pl.when(has_low_x)
    def _():
        face_copy.start()

    @pl.when(has_low_y)
    def _():
        y_copy(0, False).start()

    def pair_x(field):
        grouped = field.reshape(size_x // 2, 2, *field.shape[1:])
        return grouped[:, 0] + grouped[:, 1]

    def first_x(field):
        return field.reshape(size_x // 2, 2, *field.shape[1:])[:, 0]

    def pair_z(field):
        return jnp.stack([field[:, 0] + field[:, 1], field[:, 2] + field[:, 3]], 1)

    def first_z(field):
        return jnp.stack([field[:, 0], field[:, 2]], 1)

    def packed(field, pair_y):
        if pair_y:
            field = field + pltpu.roll(field, size_y - 1, 2)
        pairs[...] = field
        even = pairs[:, :, pl.ds(0, own_p, stride=4), :]
        odd = pairs[:, :, pl.ds(2, own_p, stride=4), :]
        return even, odd

    def put(ref, field, pair_y, scale):
        even, odd = packed(field * scale, pair_y)
        ref[:, :, 0] = even
        ref[:, :, 1] = odd

    put(coef_all.at[column, place, 0], pair_z(pair_x(alpha)), True, 0.125)
    put(coef_all.at[column, place, 1], pair_z(first_x(bx)), True, 0.0625)
    put(coef_all.at[column, place, 2], pair_z(pair_x(by)), False, 0.0625)
    put(coef_all.at[column, place, 3], first_z(pair_x(bz)), True, 0.0625)

    def row_copy(ref, ssem, rsem, other, slot):
        return pltpu.make_async_remote_copy(
            src_ref=ref.at[column, gx], dst_ref=ref.at[column, slot],
            send_sem=ssem.at[0, other], recv_sem=rsem.at[0, slot],
            device_id=(other, gy), device_id_type=MESH,
        )

    def column_copy(ref, ssem, rsem, other, slot):
        return pltpu.make_async_remote_copy(
            src_ref=ref.at[column], dst_ref=ref.at[core * chips + slot],
            send_sem=ssem.at[1, other], recv_sem=rsem.at[1, slot],
            device_id=(gx, 2 * other + core), device_id_type=MESH,
        )

    def core_copy(ref, ssem, rsem, slot):
        whole = ref.at[pl.ds(slot * chips, chips)]
        return pltpu.make_async_remote_copy(
            src_ref=whole, dst_ref=whole,
            send_sem=ssem.at[2, 0], recv_sem=rsem.at[2, 0],
            device_id=(gx, 2 * chip + 1 - core), device_id_type=MESH,
        )

    def line_copy(other, slot):
        return pltpu.make_async_remote_copy(
            src_ref=coef_all.at[column, place],
            dst_ref=coef_all.at[column, side_x * pairs_x + slot],
            send_sem=csend.at[0, other], recv_sem=crecv.at[0, slot],
            device_id=(2 * other + side_x, gy), device_id_type=MESH,
        )

    def pair_copy(side, begin, count):
        part = coef_all.at[column, pl.ds(side * pairs_x + begin, count)]
        return pltpu.make_async_remote_copy(
            src_ref=part, dst_ref=part,
            send_sem=csend.at[3, 0], recv_sem=crecv.at[3, 0],
            device_id=(2 * pos_x + 1 - side_x, gy), device_id_type=MESH,
        )

    def chip_copy(other, slot, begin, count):
        return pltpu.make_async_remote_copy(
            src_ref=coef_all.at[column, pl.ds(begin, count)],
            dst_ref=coef_all.at[core * chips + slot, pl.ds(begin, count)],
            send_sem=csend.at[1, other], recv_sem=crecv.at[1, slot],
            device_id=(gx, 2 * other + core), device_id_type=MESH,
        )

    def coef_step(half):
        if half < 2:
            middle = (pairs_x + 1) // 2
            low, high = ((1, middle), (middle, pairs_x))[half]
            each_other(pairs_x, pos_x, lambda other: line_copy(other, pos_x).start(), low, high)
        elif half < 4:
            if half == 2:
                each_other(pairs_x, pos_x, lambda other: line_copy(other, other).wait_recv())
            count = pairs_x // 2
            pair_copy(side_x, (half - 2) * count, count).start()
        elif half < 8:
            if half == 4:
                pair_copy(1 - side_x, 0, pairs_x).wait_recv()
            count = ngx // 4
            each_other(
                chips, chip,
                lambda other: chip_copy(other, chip, (half - 4) * count, count).start(),
            )

    def coef_end():
        each_other(chips, chip, lambda other: chip_copy(other, other, 0, ngx).wait_recv())
        core_copy(coef_all, csend, crecv, core).start()
        each_other(pairs_x, pos_x, lambda other: line_copy(other, pos_x).wait_send())
        pair_copy(side_x, 0, pairs_x).wait_send()
        each_other(chips, chip, lambda other: chip_copy(other, chip, 0, ngx).wait_send())
        core_copy(coef_all, csend, crecv, 1 - core).wait_recv()
        core_copy(coef_all, csend, crecv, core).wait_send()

    def each_other(count, me, action, low=1, high=None):
        def step(number, carry):
            action(lax.rem(me + number, count))
            return carry

        lax.fori_loop(low, count if high is None else high, step, 0)

    def row_start(ref, ssem, rsem):
        each_other(ngx, gx, lambda other: row_copy(ref, ssem, rsem, other, gx).start())

    def row_wait(ref, ssem, rsem):
        each_other(ngx, gx, lambda other: row_copy(ref, ssem, rsem, other, other).wait_recv())
        each_other(ngx, gx, lambda other: row_copy(ref, ssem, rsem, other, gx).wait_send())

    def column_start(ref, ssem, rsem):
        each_other(chips, chip, lambda other: column_copy(ref, ssem, rsem, other, chip).start())

    def column_wait(ref, ssem, rsem):
        each_other(chips, chip, lambda other: column_copy(ref, ssem, rsem, other, other).wait_recv())
        each_other(chips, chip, lambda other: column_copy(ref, ssem, rsem, other, chip).wait_send())

    row_y = lax.broadcasted_iota(jnp.int32, shape0, 2)
    lane = lax.broadcasted_iota(jnp.int32, shape0, 3)
    residue = lax.broadcasted_iota(jnp.int32, shape0, 1)
    row_x = lax.broadcasted_iota(jnp.int32, shape0, 0)
    offset = gx * size_x + gy * size_y
    red0 = ((row_x + residue + row_y + offset) & 1) == 0

    def z_lower(field):
        return jnp.concatenate([pltpu.roll(field[:, 3:], 1, 3), field[:, :3]], 1)

    def z_upper(field):
        return jnp.concatenate([field[:, 1:], pltpu.roll(field[:, :1], quarter - 1, 3)], 1)

    wzu = jnp.where((residue == 3) & (lane == quarter - 1), 0.0, z_upper(bz))
    l0[WZU] = wzu
    l0[WZL] = jnp.where((residue == 0) & (lane == 0), 0.0, bz)

    @pl.when(has_high_x)
    def _():
        face_copy.wait_recv()

    @pl.when(has_high_y)
    def _():
        y_copy(0, False).wait_recv()

    @pl.when(has_low_x)
    def _():
        face_copy.wait_send()

    @pl.when(has_low_y)
    def _():
        y_copy(0, False).wait_send()

    wxu = jnp.concatenate([bx[1:], bx_in[...][None]], 0)
    wyu = jnp.where(row_y == size_y - 1, hy[0, 1], pltpu.roll(by, size_y - 1, 2))
    l0[WXU] = wxu
    l0[WYU] = wyu
    diagonal = alpha + bx + wxu + by + wyu + bz + wzu
    l0[DIAG] = diagonal
    inverse = 1.0 / diagonal
    l0[INV] = inverse

    def beside0(slot):
        field = v0[...]
        below_x = jnp.concatenate([hx[0][None], field[:-1]], 0)
        above_x = jnp.concatenate([field[1:], hx[1][None]], 0)
        below_y = jnp.where(row_y == 0, hy[slot, 0], pltpu.roll(field, 1, 2))
        above_y = jnp.where(row_y == size_y - 1, hy[slot, 1], pltpu.roll(field, size_y - 1, 2))
        total = l0[WXL] * below_x + l0[WXU] * above_x
        total = total + (l0[WYL] * below_y + l0[WYU] * above_y)
        return total + (l0[WZL] * z_lower(field) + l0[WZU] * z_upper(field))

    def publish(slot, colour, field):
        v0[...] = field
        ys[slot, 0] = field[:, :, size_y - 1 :]
        ys[slot, 1] = field[:, :, 0:1]
        start_exchange(slot, colour)

    publish(1, 0, jnp.where(red0, rhs * inverse, 0.0))
    coef_step(0)
    for half in range(1, 2 * SWEEPS):
        slot = half % 2
        end_exchange(slot, (half - 1) % 2)
        updated = (l0[RHS] + beside0(slot)) * l0[INV]
        mask = red0 if half % 2 == 0 else jnp.logical_not(red0)
        if half >= 2:
            free_slot(1 - slot)
        publish(1 - slot, half % 2, jnp.where(mask, updated, v0[...]))
        coef_step(half)
    end_exchange(0, 1)
    residual0 = l0[RHS] - (l0[DIAG] * v0[...] - beside0(0))
    put(src_all.at[column, gx], pair_z(pair_x(residual0)), True, 0.125)
    row_start(src_all, gsend, grecv)
    free_slot(1)
    free_slot(0)
    coef_end()

    size_p = own_p * ngy
    shape1 = (ngx, 2, 2, 2, size_p, quarter)
    S1, INV1, DIAG1, WYL1, WZL1, UPPER1 = range(6)

    def slot_x(block):
        return lax.rem(block, 2) * pairs_x + block // 2

    def whole_field(ref, number, block):
        parts = []
        for j in range(ngy):
            k = j % 2 * chips + j // 2
            parts.append(ref[k, block] if number is None else ref[k, slot_x(block), number])
        return jnp.concatenate(parts, 3)

    wx1[ngx] = jnp.zeros(shape1[1:], F32)
    v1[...] = jnp.zeros(v1.shape, F32)
    row_p = lax.broadcasted_iota(jnp.int32, shape1[2:], 2)
    lane1 = lax.broadcasted_iota(jnp.int32, shape1[2:], 3)
    half_r = lax.broadcasted_iota(jnp.int32, shape1[2:], 0)
    half_s = lax.broadcasted_iota(jnp.int32, shape1[2:], 1)

    def coefs(block, carry):
        wx1[block] = whole_field(coef_all, 1, block)
        return carry

    lax.fori_loop(0, ngx, coefs, 0)

    def more_coefs(block, carry):
        a1 = whole_field(coef_all, 0, block)
        lower_x = wx1[block]
        next_x = wx1[block + 1]
        upper_x = jnp.stack([lower_x[1], next_x[0]], 0)
        lower_y = whole_field(coef_all, 2, block)
        upper_y = jnp.stack([lower_y[:, :, 1], pltpu.roll(lower_y[:, :, 0], size_p - 1, 2)], 2)
        upper_y = jnp.where((half_s == 1) & (row_p == size_p - 1), 0.0, upper_y)
        lower_z = whole_field(coef_all, 3, block)
        upper_z = jnp.stack([lower_z[:, 1], pltpu.roll(lower_z[:, 0], quarter - 1, 3)], 1)
        upper_z = jnp.where((half_r == 1) & (lane1 == quarter - 1), 0.0, upper_z)
        diagonal1 = a1 + lower_x + upper_x + lower_y + upper_y + lower_z + upper_z
        l1[DIAG1, block] = diagonal1
        l1[INV1, block] = 1.0 / diagonal1
        l1[WYL1, block] = lower_y
        l1[UPPER1, block, :, 0] = upper_y[:, :, 1]
        l1[WZL1, block] = lower_z
        l1[UPPER1, block, :, 1] = upper_z[:, 1]
        return carry

    lax.fori_loop(0, ngx, more_coefs, 0)

    shape2 = (ngx, size_p, quarter)
    row2 = lax.broadcasted_iota(jnp.int32, shape2, 1)
    lane2 = lax.broadcasted_iota(jnp.int32, shape2, 2)
    block2 = lax.broadcasted_iota(jnp.int32, shape2, 0)
    red2 = ((block2 + row2 + lane2) & 1) == 0

    def summed(ref, fixed):
        total = None
        for xl in (0, 1):
            for r in (0, 1):
                for s in (0, 1):
                    if (xl, r, s)[fixed] == 0:
                        term = ref(xl, r, s)
                        total = term if total is None else total + term
        return total

    a2_parts = None
    for j in range(ngy):
        k = j % 2 * chips + j // 2
        part = None
        for xl in (0, 1):
            for r in (0, 1):
                for s in (0, 1):
                    term = jnp.stack(
                        [coef_all[k, b % 2 * pairs_x + b // 2, 0, xl, r, s] for b in range(ngx)], 0
                    )
                    part = term if part is None else part + term
        a2_parts = [part] if a2_parts is None else a2_parts + [part]
    a2 = jnp.concatenate(a2_parts, 1) * 0.125
    lower_x2 = summed(lambda xl, r, s: wx1[0:ngx, xl, r, s], 0) * 0.0625
    lower_y2 = summed(lambda xl, r, s: l1[WYL1, :, xl, r, s], 2) * 0.0625
    lower_z2 = summed(lambda xl, r, s: l1[WZL1, :, xl, r, s], 1) * 0.0625
    upper_x2 = jnp.concatenate([lower_x2[1:], jnp.zeros((1, size_p, quarter), F32)], 0)
    upper_y2 = jnp.where(row2 == size_p - 1, 0.0, pltpu.roll(lower_y2, size_p - 1, 1))
    upper_z2 = jnp.where(lane2 == quarter - 1, 0.0, pltpu.roll(lower_z2, quarter - 1, 2))
    diagonal2 = a2 + lower_x2 + upper_x2 + lower_y2 + upper_y2 + lower_z2 + upper_z2
    A2, WXL2, WXU2, WYL2, WYU2, WZL2, WZU2 = range(7)
    c2[A2] = 1.0 / diagonal2
    c2[WXL2] = lower_x2
    c2[WXU2] = upper_x2
    c2[WYL2] = jnp.where(row2 == 0, 0.0, lower_y2)
    c2[WYU2] = upper_y2
    c2[WZL2] = jnp.where(lane2 == 0, 0.0, lower_z2)
    c2[WZU2] = upper_z2
    for xl in (0, 1):
        for r in (0, 1):
            l1[WYL1, :, xl, r, 0] = jnp.where(row2 == 0, 0.0, l1[WYL1, :, xl, r, 0])
        for s in (0, 1):
            l1[WZL1, :, xl, 0, s] = jnp.where(lane2 == 0, 0.0, l1[WZL1, :, xl, 0, s])

    row_wait(src_all, gsend, grecv)
    column_start(src_all, gsend, grecv)
    column_wait(src_all, gsend, grecv)
    core_copy(src_all, gsend, grecv, core).start()
    core_copy(src_all, gsend, grecv, 1 - core).wait_recv()

    for block in range(ngx):
        l1[S1, block] = whole_field(src_all, None, block)

    def beside1(xl, r, s):
        if xl == 0:
            below_x = v1[0:ngx, 1, r, s]
            above_x = v1[1 : ngx + 1, 1, r, s]
            face_above = wx1[0:ngx, 1, r, s]
        else:
            below_x = v1[1 : ngx + 1, 0, r, s]
            above_x = v1[2 : ngx + 2, 0, r, s]
            face_above = wx1[1 : ngx + 1, 0, r, s]
        side_y = v1[1 : ngx + 1, xl, r, 1 - s]
        side_z = v1[1 : ngx + 1, xl, 1 - r, s]
        below_y = pltpu.roll(side_y, 1, 1) if s == 0 else side_y
        above_y = side_y if s == 0 else pltpu.roll(side_y, size_p - 1, 1)
        below_z = pltpu.roll(side_z, 1, 2) if r == 0 else side_z
        above_z = side_z if r == 0 else pltpu.roll(side_z, quarter - 1, 2)
        total = wx1[0:ngx, xl, r, s] * below_x + face_above * above_x
        upper_y = l1[WYL1, :, xl, r, 1] if s == 0 else l1[UPPER1, :, xl, 0, r]
        upper_z = l1[WZL1, :, xl, 1, s] if r == 0 else l1[UPPER1, :, xl, 1, s]
        total = total + (l1[WYL1, :, xl, r, s] * below_y + upper_y * above_y)
        return total + (l1[WZL1, :, xl, r, s] * below_z + upper_z * above_z)

    def half1(colour):
        for xl in (0, 1):
            for r in (0, 1):
                s = (xl + r + colour) % 2
                v1[1 : ngx + 1, xl, r, s] = (
                    l1[S1, :, xl, r, s] + beside1(xl, r, s)
                ) * l1[INV1, :, xl, r, s]

    def sweep1(number, carry):
        half1(0)
        half1(1)
        return carry

    lax.fori_loop(0, SWEEPS, sweep1, 0)

    source2 = None
    for xl in (0, 1):
        for r in (0, 1):
            for s in (0, 1):
                term = l1[S1, :, xl, r, s] - (
                    l1[DIAG1, :, xl, r, s] * v1[1 : ngx + 1, xl, r, s] - beside1(xl, r, s)
                )
                source2 = term if source2 is None else source2 + term
    source2 = source2 * 0.125

    zero_block = jnp.zeros((1, size_p, quarter), F32)

    def half2(field, mask):
        below_x = jnp.concatenate([zero_block, field[:-1]], 0)
        above_x = jnp.concatenate([field[1:], zero_block], 0)
        total = c2[WXL2] * below_x + c2[WXU2] * above_x
        total = total + (
            c2[WYL2] * pltpu.roll(field, 1, 1) + c2[WYU2] * pltpu.roll(field, size_p - 1, 1)
        )
        total = total + (
            c2[WZL2] * pltpu.roll(field, 1, 2) + c2[WZU2] * pltpu.roll(field, quarter - 1, 2)
        )
        return jnp.where(mask, (source2 + total) * c2[A2], field)

    def sweep2(number, field):
        return half2(half2(field, red2), jnp.logical_not(red2))

    core_copy(src_all, gsend, grecv, core).wait_send()
    coarse = lax.fori_loop(0, COARSE_SWEEPS, sweep2, jnp.zeros(shape2, F32))
    c2[A2] = coarse

    shift = lax.rem(size_p - own_p * gy, size_p)
    own_coarse = c2[A2, gx]
    coarse_ref[0] = pltpu.roll(own_coarse, shift, 0)[:own_p]
    for xl in (0, 1):
        for r in (0, 1):
            for s in (0, 1):
                tile = pltpu.roll(v1[gx + 1, xl, r, s] + own_coarse, shift, 0)[:own_p]
                spread[xl, r, pl.ds(2 * s, own_p, stride=4), :] = tile
                spread[xl, r, pl.ds(2 * s + 1, own_p, stride=4), :] = tile
    added = []
    for x in range(size_x):
        added.append(jnp.concatenate([v0[x, r] + spread[x // 2, r // 2] for r in range(4)], 1))
    natural = permuted(jnp.concatenate(added, 0), order[...], True)
    fine_ref[...] = natural.reshape(size_x, size_y, size_z)


def on_device(ngx, ngy, rhs, alpha, beta_x, beta_y, beta_z):
    size_x, size_y, size_z = rhs.shape
    quarter = size_z // 4
    own_p = size_y // 4
    size_p = own_p * ngy
    field0 = (size_x, 4, size_y, quarter)
    block1 = (2, 2, 2, size_p, quarter)
    piece1 = (2, 2, 2, own_p, quarter)
    dma = pltpu.SemaphoreType.DMA
    most = max(ngx, ngy)
    return pl.pallas_call(
        functools.partial(kernel, ngx, ngy),
        out_shape=(
            jax.ShapeDtypeStruct(rhs.shape, F32),
            jax.ShapeDtypeStruct((size_x // 4, own_p, quarter), F32),
        ),
        in_specs=[pl.BlockSpec(memory_space=pltpu.VMEM)] * 5,
        out_specs=(pl.BlockSpec(memory_space=pltpu.VMEM),) * 2,
        scratch_shapes=[
            pltpu.VMEM((9,) + field0, F32),
            pltpu.VMEM(field0, F32),
            pltpu.VMEM((2,) + field0[1:], F32),
            pltpu.VMEM(field0[1:], F32),
            pltpu.VMEM((2, 2, 4, size_y // 2, quarter), F32),
            pltpu.VMEM((2, 2, 4, size_y // 2, quarter), F32),
            pltpu.VMEM((2, 2, size_x, 4, 1, quarter), F32),
            pltpu.VMEM((2, 2, size_x, 4, 1, quarter), F32),
            pltpu.VMEM((size_x // 2, 2, size_y, quarter), F32),
            pltpu.VMEM((ngy, ngx) + piece1, F32),
            pltpu.VMEM((ngy, ngx, 4) + piece1, F32),
            pltpu.VMEM((6, ngx) + block1, F32),
            pltpu.VMEM((ngx + 1,) + block1, F32),
            pltpu.VMEM((ngx + 2,) + block1, F32),
            pltpu.VMEM((7, ngx, size_p, quarter), F32),
            pltpu.VMEM((2, 2, size_y, quarter), F32),
            pltpu.VMEM((size_z, size_z), jnp.bfloat16),
            dma((3, 2)), dma((3, 2)), dma((2, 2)), dma((2, 2)),
            dma((3, most)), dma((3, most)), dma((4, most)), dma((4, most)),
        ],
        compiler_params=pltpu.CompilerParams(
            collective_id=0, has_side_effects=True, vmem_limit_bytes=62 * 1024 * 1024
        ),
    )(rhs, alpha, beta_x, beta_y, beta_z)


def solution(mesh):
    spec = P("gx", "gy", None)
    return jax.shard_map(
        functools.partial(on_device, mesh.shape["gx"], mesh.shape["gy"]),
        mesh=mesh,
        in_specs=(spec,) * 5,
        out_specs=(spec, spec),
        check_vma=False,
    )
```

```python
import functools

import jax
import jax.numpy as jnp
from jax import lax
from jax.experimental import pallas as pl
from jax.experimental.pallas import tpu as pltpu
from jax.sharding import PartitionSpec as P

SWEEPS = 4
COARSE_SWEEPS = 8
MESH = pl.DeviceIdType.MESH
F32 = jnp.float32
LANES = 128


def order_matrix(size):
    quarter = size // 4
    row = lax.broadcasted_iota(jnp.int32, (size, quarter), 0)
    col = lax.broadcasted_iota(jnp.int32, (size, quarter), 1)
    difference = row - 4 * col
    return jnp.concatenate(
        [jnp.where(difference == r, 1.0, 0.0).astype(jnp.bfloat16) for r in range(4)], 1
    )


def permuted(rows, matrix, back):
    count = rows.shape[0]
    high = rows.astype(jnp.bfloat16)
    rest = rows - high.astype(F32)
    middle = rest.astype(jnp.bfloat16)
    low = (rest - middle.astype(F32)).astype(jnp.bfloat16)
    stacked = jnp.concatenate([high, middle, low], 0)
    out = lax.dot_general(
        stacked, matrix, (((1,), (1 if back else 0,)), ((), ())), preferred_element_type=F32
    )
    return (out[2 * count :] + out[count : 2 * count]) + out[:count]


def kernel(
    ngx, ngy,
    rhs_ref, alpha_ref, bx_ref, by_ref, bz_ref,
    fine_ref, coarse_ref,
    l0, v0, hx, bx_in, px, qx, ys, hy, pairs, src_all, coef_all, l1, wx1, v1, c2, spread, order,
    xsend, xrecv, ysend, yrecv, gsend, grecv, csend, crecv,
):
    gx = lax.axis_index("gx")
    gy = lax.axis_index("gy")
    size_x, size_y, size_z = rhs_ref.shape
    quarter = size_z // 4
    own_p = size_y // 4
    chips, chip, core = ngy // 2, gy // 2, lax.rem(gy, 2)
    column = core * chips + chip
    pairs_x, pos_x, side_x = ngx // 2, gx // 2, lax.rem(gx, 2)
    place = side_x * pairs_x + pos_x
    shape0 = (size_x, 4, size_y, quarter)

    hx[...] = jnp.zeros(hx.shape, F32)
    bx_in[...] = jnp.zeros(bx_in.shape, F32)
    hy[...] = jnp.zeros(hy.shape, F32)

    barrier = pltpu.get_barrier_semaphore()

    def greet_x(step, carry):
        other = lax.rem(gx + step, ngx)
        pl.semaphore_signal(barrier, inc=1, device_id=(other, gy), device_id_type=MESH)
        return carry

    def greet_y(step, carry):
        other = lax.rem(gy + step, ngy)
        pl.semaphore_signal(barrier, inc=1, device_id=(gx, other), device_id_type=MESH)
        return carry

    lax.fori_loop(1, ngx, greet_x, 0)
    lax.fori_loop(1, ngy, greet_y, 0)

    matrix = order_matrix(size_z)
    order[...] = matrix
    rows = size_x * size_y
    stacked = jnp.concatenate(
        [ref[...].reshape(rows, size_z) for ref in (rhs_ref, alpha_ref, bx_ref, by_ref, bz_ref)], 0
    )
    ordered = permuted(stacked, matrix, False)

    def ordered_field(number):
        whole = ordered[number * rows : (number + 1) * rows].reshape(size_x, size_y, size_z)
        return jnp.stack([whole[:, :, r * quarter : (r + 1) * quarter] for r in range(4)], 1)

    rhs, alpha, bx, by, bz = [ordered_field(number) for number in range(5)]
    RHS, INV, DIAG, WXL, WXU, WYL, WYU, WZL, WZU = range(9)
    l0[RHS] = rhs
    l0[WXL] = bx
    l0[WYL] = by

    pl.semaphore_wait(barrier, ngx - 1 + ngy - 1)

    def x_copy(slot, up):
        side = 0 if up else 1
        return pltpu.make_async_remote_copy(
            src_ref=px.at[slot, side],
            dst_ref=qx.at[slot, side],
            send_sem=xsend.at[slot, side],
            recv_sem=xrecv.at[slot, side],
            device_id=(gx + 1 if up else gx - 1, gy),
            device_id_type=MESH,
        )

    def y_copy(slot, up):
        side = 0 if up else 1
        return pltpu.make_async_remote_copy(
            src_ref=ys.at[slot, side],
            dst_ref=hy.at[slot, side],
            send_sem=ysend.at[slot, side],
            recv_sem=yrecv.at[slot, side],
            device_id=(gx, gy + 1 if up else gy - 1),
            device_id_type=MESH,
        )

    face_copy = pltpu.make_async_remote_copy(
        src_ref=l0.at[WXL, 0],
        dst_ref=bx_in,
        send_sem=xsend.at[2, 0],
        recv_sem=xrecv.at[2, 0],
        device_id=(gx - 1, gy),
        device_id_type=MESH,
    )

    has_low_x, has_high_x = gx > 0, gx < ngx - 1
    has_low_y, has_high_y = gy > 0, gy < ngy - 1

    def strided(colour, up, r):
        x = size_x - 1 if up else 0
        return pl.ds((colour + x + r) % 2, size_y // 2, stride=2)

    def start_exchange(slot, colour):
        for up in (False, True):
            side = 0 if up else 1
            plane = size_x - 1 if up else 0

            @pl.when(has_high_x if up else has_low_x)
            def _():
                for r in range(4):
                    px[slot, side, r] = v0[plane, r, strided(colour, up, r), :]
                x_copy(slot, up).start()
        for up in (False, True):
            @pl.when(has_high_y if up else has_low_y)
            def _():
                y_copy(slot, up).start()

    def end_exchange(slot, colour):
        for up in (False, True):
            side = 0 if up else 1

            @pl.when(has_low_y if up else has_high_y)
            def _():
                y_copy(slot, up).wait_recv()

            @pl.when(has_low_x if up else has_high_x)
            def _():
                x_copy(slot, up).wait_recv()
                for r in range(4):
                    hx[side, r, strided(colour, up, r), :] = qx[slot, side, r]

    def free_slot(slot):
        for up in (False, True):
            @pl.when(has_high_x if up else has_low_x)
            def _():
                x_copy(slot, up).wait_send()

            @pl.when(has_high_y if up else has_low_y)
            def _():
                y_copy(slot, up).wait_send()

    ys[0, 1] = by[:, :, 0:1]

    @pl.when(has_low_x)
    def _():
        face_copy.start()

    @pl.when(has_low_y)
    def _():
        y_copy(0, False).start()

    def pair_x(field):
        grouped = field.reshape(size_x // 2, 2, *field.shape[1:])
        return grouped[:, 0] + grouped[:, 1]

    def first_x(field):
        return field.reshape(size_x // 2, 2, *field.shape[1:])[:, 0]

    def pair_z(field):
        return jnp.stack([field[:, 0] + field[:, 1], field[:, 2] + field[:, 3]], 1)

    def first_z(field):
        return jnp.stack([field[:, 0], field[:, 2]], 1)

    def packed(field, pair_y):
        if pair_y:
            field = field + pltpu.roll(field, size_y - 1, 2)
        pairs[...] = field
        even = pairs[:, :, pl.ds(0, own_p, stride=4), :]
        odd = pairs[:, :, pl.ds(2, own_p, stride=4), :]
        return even, odd

    def put(ref, field, pair_y, scale):
        even, odd = packed(field * scale, pair_y)
        ref[:, :, 0] = even
        ref[:, :, 1] = odd

    put(coef_all.at[column, place, 0], pair_z(pair_x(alpha)), True, 0.125)
    put(coef_all.at[column, place, 1], pair_z(first_x(bx)), True, 0.0625)
    put(coef_all.at[column, place, 2], pair_z(pair_x(by)), False, 0.0625)
    put(coef_all.at[column, place, 3], first_z(pair_x(bz)), True, 0.0625)

    def row_copy(ref, ssem, rsem, other, slot):
        return pltpu.make_async_remote_copy(
            src_ref=ref.at[column, gx], dst_ref=ref.at[column, slot],
            send_sem=ssem.at[0, other], recv_sem=rsem.at[0, slot],
            device_id=(other, gy), device_id_type=MESH,
        )

    def column_copy(ref, ssem, rsem, other, slot):
        return pltpu.make_async_remote_copy(
            src_ref=ref.at[column], dst_ref=ref.at[core * chips + slot],
            send_sem=ssem.at[1, other], recv_sem=rsem.at[1, slot],
            device_id=(gx, 2 * other + core), device_id_type=MESH,
        )

    def core_copy(ref, ssem, rsem, slot):
        whole = ref.at[pl.ds(slot * chips, chips)]
        return pltpu.make_async_remote_copy(
            src_ref=whole, dst_ref=whole,
            send_sem=ssem.at[2, 0], recv_sem=rsem.at[2, 0],
            device_id=(gx, 2 * chip + 1 - core), device_id_type=MESH,
        )

    def line_copy(other, slot):
        return pltpu.make_async_remote_copy(
            src_ref=coef_all.at[column, place],
            dst_ref=coef_all.at[column, side_x * pairs_x + slot],
            send_sem=csend.at[0, other], recv_sem=crecv.at[0, slot],
            device_id=(2 * other + side_x, gy), device_id_type=MESH,
        )

    def pair_copy(side, begin, count):
        part = coef_all.at[column, pl.ds(side * pairs_x + begin, count)]
        return pltpu.make_async_remote_copy(
            src_ref=part, dst_ref=part,
            send_sem=csend.at[3, 0], recv_sem=crecv.at[3, 0],
            device_id=(2 * pos_x + 1 - side_x, gy), device_id_type=MESH,
        )

    def chip_copy(other, slot, begin, count):
        return pltpu.make_async_remote_copy(
            src_ref=coef_all.at[column, pl.ds(begin, count)],
            dst_ref=coef_all.at[core * chips + slot, pl.ds(begin, count)],
            send_sem=csend.at[1, other], recv_sem=crecv.at[1, slot],
            device_id=(gx, 2 * other + core), device_id_type=MESH,
        )

    def coef_step(half):
        if half < 2:
            middle = (pairs_x + 1) // 2
            low, high = ((1, middle), (middle, pairs_x))[half]
            each_other(pairs_x, pos_x, lambda other: line_copy(other, pos_x).start(), low, high)
        elif half < 4:
            if half == 2:
                each_other(pairs_x, pos_x, lambda other: line_copy(other, other).wait_recv())
            count = pairs_x // 2
            pair_copy(side_x, (half - 2) * count, count).start()
        elif half < 8:
            if half == 4:
                pair_copy(1 - side_x, 0, pairs_x).wait_recv()
            count = ngx // 4
            each_other(
                chips, chip,
                lambda other: chip_copy(other, chip, (half - 4) * count, count).start(),
            )

    def coef_end():
        each_other(chips, chip, lambda other: chip_copy(other, other, 0, ngx).wait_recv())
        core_copy(coef_all, csend, crecv, core).start()
        each_other(pairs_x, pos_x, lambda other: line_copy(other, pos_x).wait_send())
        pair_copy(side_x, 0, pairs_x).wait_send()
        each_other(chips, chip, lambda other: chip_copy(other, chip, 0, ngx).wait_send())
        core_copy(coef_all, csend, crecv, 1 - core).wait_recv()
        core_copy(coef_all, csend, crecv, core).wait_send()

    def each_other(count, me, action, low=1, high=None):
        def step(number, carry):
            action(lax.rem(me + number, count))
            return carry

        lax.fori_loop(low, count if high is None else high, step, 0)

    def row_start(ref, ssem, rsem):
        each_other(ngx, gx, lambda other: row_copy(ref, ssem, rsem, other, gx).start())

    def row_wait(ref, ssem, rsem):
        each_other(ngx, gx, lambda other: row_copy(ref, ssem, rsem, other, other).wait_recv())
        each_other(ngx, gx, lambda other: row_copy(ref, ssem, rsem, other, gx).wait_send())

    def column_start(ref, ssem, rsem):
        each_other(chips, chip, lambda other: column_copy(ref, ssem, rsem, other, chip).start())

    def column_wait(ref, ssem, rsem):
        each_other(chips, chip, lambda other: column_copy(ref, ssem, rsem, other, other).wait_recv())
        each_other(chips, chip, lambda other: column_copy(ref, ssem, rsem, other, chip).wait_send())

    row_y = lax.broadcasted_iota(jnp.int32, shape0, 2)
    lane = lax.broadcasted_iota(jnp.int32, shape0, 3)
    residue = lax.broadcasted_iota(jnp.int32, shape0, 1)
    row_x = lax.broadcasted_iota(jnp.int32, shape0, 0)
    offset = gx * size_x + gy * size_y
    red0 = ((row_x + residue + row_y + offset) & 1) == 0

    def z_lower(field):
        return jnp.concatenate([pltpu.roll(field[:, 3:], 1, 3), field[:, :3]], 1)

    def z_upper(field):
        return jnp.concatenate([field[:, 1:], pltpu.roll(field[:, :1], quarter - 1, 3)], 1)

    wzu = jnp.where((residue == 3) & (lane == quarter - 1), 0.0, z_upper(bz))
    l0[WZU] = wzu
    l0[WZL] = jnp.where((residue == 0) & (lane == 0), 0.0, bz)

    @pl.when(has_high_x)
    def _():
        face_copy.wait_recv()

    @pl.when(has_high_y)
    def _():
        y_copy(0, False).wait_recv()

    @pl.when(has_low_x)
    def _():
        face_copy.wait_send()

    @pl.when(has_low_y)
    def _():
        y_copy(0, False).wait_send()

    wxu = jnp.concatenate([bx[1:], bx_in[...][None]], 0)
    wyu = jnp.where(row_y == size_y - 1, hy[0, 1], pltpu.roll(by, size_y - 1, 2))
    l0[WXU] = wxu
    l0[WYU] = wyu
    diagonal = alpha + bx + wxu + by + wyu + bz + wzu
    l0[DIAG] = diagonal
    inverse = 1.0 / diagonal
    l0[INV] = inverse

    def beside0(slot):
        field = v0[...]
        below_x = jnp.concatenate([hx[0][None], field[:-1]], 0)
        above_x = jnp.concatenate([field[1:], hx[1][None]], 0)
        below_y = jnp.where(row_y == 0, hy[slot, 0], pltpu.roll(field, 1, 2))
        above_y = jnp.where(row_y == size_y - 1, hy[slot, 1], pltpu.roll(field, size_y - 1, 2))
        total = l0[WXL] * below_x + l0[WXU] * above_x
        total = total + (l0[WYL] * below_y + l0[WYU] * above_y)
        return total + (l0[WZL] * z_lower(field) + l0[WZU] * z_upper(field))

    def publish(slot, colour, field):
        v0[...] = field
        ys[slot, 0] = field[:, :, size_y - 1 :]
        ys[slot, 1] = field[:, :, 0:1]
        start_exchange(slot, colour)

    publish(1, 0, jnp.where(red0, rhs * inverse, 0.0))
    coef_step(0)
    for half in range(1, 2 * SWEEPS):
        slot = half % 2
        end_exchange(slot, (half - 1) % 2)
        updated = (l0[RHS] + beside0(slot)) * l0[INV]
        mask = red0 if half % 2 == 0 else jnp.logical_not(red0)
        if half >= 2:
            free_slot(1 - slot)
        publish(1 - slot, half % 2, jnp.where(mask, updated, v0[...]))
        coef_step(half)
    end_exchange(0, 1)
    residual0 = l0[RHS] - (l0[DIAG] * v0[...] - beside0(0))
    put(src_all.at[column, gx], pair_z(pair_x(residual0)), True, 0.125)
    row_start(src_all, gsend, grecv)
    free_slot(1)
    free_slot(0)
    coef_end()
    row_wait(src_all, gsend, grecv)
    column_start(src_all, gsend, grecv)

    size_p = own_p * ngy
    shape1 = (ngx, 2, 2, 2, size_p, quarter)
    S1, INV1, DIAG1, WYL1, WZL1, UPPER1 = range(6)

    def slot_x(block):
        return lax.rem(block, 2) * pairs_x + block // 2

    def whole_field(ref, number, block):
        parts = []
        for j in range(ngy):
            k = j % 2 * chips + j // 2
            parts.append(ref[k, block] if number is None else ref[k, slot_x(block), number])
        return jnp.concatenate(parts, 3)

    wx1[ngx] = jnp.zeros(shape1[1:], F32)
    v1[...] = jnp.zeros(v1.shape, F32)
    row_p = lax.broadcasted_iota(jnp.int32, shape1[2:], 2)
    lane1 = lax.broadcasted_iota(jnp.int32, shape1[2:], 3)
    half_r = lax.broadcasted_iota(jnp.int32, shape1[2:], 0)
    half_s = lax.broadcasted_iota(jnp.int32, shape1[2:], 1)

    def coefs(block, carry):
        wx1[block] = whole_field(coef_all, 1, block)
        return carry

    lax.fori_loop(0, ngx, coefs, 0)

    def more_coefs(block, carry):
        a1 = whole_field(coef_all, 0, block)
        lower_x = wx1[block]
        next_x = wx1[block + 1]
        upper_x = jnp.stack([lower_x[1], next_x[0]], 0)
        lower_y = whole_field(coef_all, 2, block)
        upper_y = jnp.stack([lower_y[:, :, 1], pltpu.roll(lower_y[:, :, 0], size_p - 1, 2)], 2)
        upper_y = jnp.where((half_s == 1) & (row_p == size_p - 1), 0.0, upper_y)
        lower_z = whole_field(coef_all, 3, block)
        upper_z = jnp.stack([lower_z[:, 1], pltpu.roll(lower_z[:, 0], quarter - 1, 3)], 1)
        upper_z = jnp.where((half_r == 1) & (lane1 == quarter - 1), 0.0, upper_z)
        diagonal1 = a1 + lower_x + upper_x + lower_y + upper_y + lower_z + upper_z
        l1[DIAG1, block] = diagonal1
        l1[INV1, block] = 1.0 / diagonal1
        l1[WYL1, block] = lower_y
        l1[UPPER1, block, :, 0] = upper_y[:, :, 1]
        l1[WZL1, block] = lower_z
        l1[UPPER1, block, :, 1] = upper_z[:, 1]
        return carry

    def two_blocks(number, carry):
        return more_coefs(2 * number + 1, more_coefs(2 * number, carry))

    lax.fori_loop(0, ngx // 2, two_blocks, 0)
    column_wait(src_all, gsend, grecv)
    core_copy(src_all, gsend, grecv, core).start()

    shape2 = (ngx, size_p, quarter)
    row2 = lax.broadcasted_iota(jnp.int32, shape2, 1)
    lane2 = lax.broadcasted_iota(jnp.int32, shape2, 2)
    block2 = lax.broadcasted_iota(jnp.int32, shape2, 0)
    red2 = ((block2 + row2 + lane2) & 1) == 0

    def summed(ref, fixed):
        total = None
        for xl in (0, 1):
            for r in (0, 1):
                for s in (0, 1):
                    if (xl, r, s)[fixed] == 0:
                        term = ref(xl, r, s)
                        total = term if total is None else total + term
        return total

    a2_parts = None
    for j in range(ngy):
        k = j % 2 * chips + j // 2
        part = None
        for xl in (0, 1):
            for r in (0, 1):
                for s in (0, 1):
                    term = jnp.stack(
                        [coef_all[k, b % 2 * pairs_x + b // 2, 0, xl, r, s] for b in range(ngx)], 0
                    )
                    part = term if part is None else part + term
        a2_parts = [part] if a2_parts is None else a2_parts + [part]
    a2 = jnp.concatenate(a2_parts, 1) * 0.125
    lower_x2 = summed(lambda xl, r, s: wx1[0:ngx, xl, r, s], 0) * 0.0625
    lower_y2 = summed(lambda xl, r, s: l1[WYL1, :, xl, r, s], 2) * 0.0625
    lower_z2 = summed(lambda xl, r, s: l1[WZL1, :, xl, r, s], 1) * 0.0625
    upper_x2 = jnp.concatenate([lower_x2[1:], jnp.zeros((1, size_p, quarter), F32)], 0)
    upper_y2 = jnp.where(row2 == size_p - 1, 0.0, pltpu.roll(lower_y2, size_p - 1, 1))
    upper_z2 = jnp.where(lane2 == quarter - 1, 0.0, pltpu.roll(lower_z2, quarter - 1, 2))
    diagonal2 = a2 + lower_x2 + upper_x2 + lower_y2 + upper_y2 + lower_z2 + upper_z2
    A2, WXL2, WXU2, WYL2, WYU2, WZL2, WZU2 = range(7)
    c2[A2] = 1.0 / diagonal2
    c2[WXL2] = lower_x2
    c2[WXU2] = upper_x2
    c2[WYL2] = jnp.where(row2 == 0, 0.0, lower_y2)
    c2[WYU2] = upper_y2
    c2[WZL2] = jnp.where(lane2 == 0, 0.0, lower_z2)
    c2[WZU2] = upper_z2
    for xl in (0, 1):
        for r in (0, 1):
            l1[WYL1, :, xl, r, 0] = jnp.where(row2 == 0, 0.0, l1[WYL1, :, xl, r, 0])
        for s in (0, 1):
            l1[WZL1, :, xl, 0, s] = jnp.where(lane2 == 0, 0.0, l1[WZL1, :, xl, 0, s])

    core_copy(src_all, gsend, grecv, 1 - core).wait_recv()

    for block in range(ngx):
        l1[S1, block] = whole_field(src_all, None, block)

    def beside1(xl, r, s):
        if xl == 0:
            below_x = v1[0:ngx, 1, r, s]
            above_x = v1[1 : ngx + 1, 1, r, s]
            face_above = wx1[0:ngx, 1, r, s]
        else:
            below_x = v1[1 : ngx + 1, 0, r, s]
            above_x = v1[2 : ngx + 2, 0, r, s]
            face_above = wx1[1 : ngx + 1, 0, r, s]
        side_y = v1[1 : ngx + 1, xl, r, 1 - s]
        side_z = v1[1 : ngx + 1, xl, 1 - r, s]
        below_y = pltpu.roll(side_y, 1, 1) if s == 0 else side_y
        above_y = side_y if s == 0 else pltpu.roll(side_y, size_p - 1, 1)
        below_z = pltpu.roll(side_z, 1, 2) if r == 0 else side_z
        above_z = side_z if r == 0 else pltpu.roll(side_z, quarter - 1, 2)
        total = wx1[0:ngx, xl, r, s] * below_x + face_above * above_x
        upper_y = l1[WYL1, :, xl, r, 1] if s == 0 else l1[UPPER1, :, xl, 0, r]
        upper_z = l1[WZL1, :, xl, 1, s] if r == 0 else l1[UPPER1, :, xl, 1, s]
        total = total + (l1[WYL1, :, xl, r, s] * below_y + upper_y * above_y)
        return total + (l1[WZL1, :, xl, r, s] * below_z + upper_z * above_z)

    def half1(colour):
        for xl in (0, 1):
            for r in (0, 1):
                s = (xl + r + colour) % 2
                v1[1 : ngx + 1, xl, r, s] = (
                    l1[S1, :, xl, r, s] + beside1(xl, r, s)
                ) * l1[INV1, :, xl, r, s]

    def sweep1(number, carry):
        half1(0)
        half1(1)
        return carry

    lax.fori_loop(0, SWEEPS, sweep1, 0)

    source2 = None
    for xl in (0, 1):
        for r in (0, 1):
            for s in (0, 1):
                term = l1[S1, :, xl, r, s] - (
                    l1[DIAG1, :, xl, r, s] * v1[1 : ngx + 1, xl, r, s] - beside1(xl, r, s)
                )
                source2 = term if source2 is None else source2 + term
    source2 = source2 * 0.125

    zero_block = jnp.zeros((1, size_p, quarter), F32)

    def half2(field, mask):
        below_x = jnp.concatenate([zero_block, field[:-1]], 0)
        above_x = jnp.concatenate([field[1:], zero_block], 0)
        total = c2[WXL2] * below_x + c2[WXU2] * above_x
        total = total + (
            c2[WYL2] * pltpu.roll(field, 1, 1) + c2[WYU2] * pltpu.roll(field, size_p - 1, 1)
        )
        total = total + (
            c2[WZL2] * pltpu.roll(field, 1, 2) + c2[WZU2] * pltpu.roll(field, quarter - 1, 2)
        )
        return jnp.where(mask, (source2 + total) * c2[A2], field)

    def sweep2(number, field):
        return half2(half2(field, red2), jnp.logical_not(red2))

    core_copy(src_all, gsend, grecv, core).wait_send()
    coarse = lax.fori_loop(0, COARSE_SWEEPS, sweep2, jnp.zeros(shape2, F32))
    c2[A2] = coarse

    shift = lax.rem(size_p - own_p * gy, size_p)
    own_coarse = c2[A2, gx]
    coarse_ref[0] = pltpu.roll(own_coarse, shift, 0)[:own_p]
    for xl in (0, 1):
        for r in (0, 1):
            for s in (0, 1):
                tile = pltpu.roll(v1[gx + 1, xl, r, s] + own_coarse, shift, 0)[:own_p]
                spread[xl, r, pl.ds(2 * s, own_p, stride=4), :] = tile
                spread[xl, r, pl.ds(2 * s + 1, own_p, stride=4), :] = tile
    added = []
    for x in range(size_x):
        added.append(jnp.concatenate([v0[x, r] + spread[x // 2, r // 2] for r in range(4)], 1))
    natural = permuted(jnp.concatenate(added, 0), order[...], True)
    fine_ref[...] = natural.reshape(size_x, size_y, size_z)


def on_device(ngx, ngy, rhs, alpha, beta_x, beta_y, beta_z):
    size_x, size_y, size_z = rhs.shape
    quarter = size_z // 4
    own_p = size_y // 4
    size_p = own_p * ngy
    field0 = (size_x, 4, size_y, quarter)
    block1 = (2, 2, 2, size_p, quarter)
    piece1 = (2, 2, 2, own_p, quarter)
    dma = pltpu.SemaphoreType.DMA
    most = max(ngx, ngy)
    return pl.pallas_call(
        functools.partial(kernel, ngx, ngy),
        out_shape=(
            jax.ShapeDtypeStruct(rhs.shape, F32),
            jax.ShapeDtypeStruct((size_x // 4, own_p, quarter), F32),
        ),
        in_specs=[pl.BlockSpec(memory_space=pltpu.VMEM)] * 5,
        out_specs=(pl.BlockSpec(memory_space=pltpu.VMEM),) * 2,
        scratch_shapes=[
            pltpu.VMEM((9,) + field0, F32),
            pltpu.VMEM(field0, F32),
            pltpu.VMEM((2,) + field0[1:], F32),
            pltpu.VMEM(field0[1:], F32),
            pltpu.VMEM((2, 2, 4, size_y // 2, quarter), F32),
            pltpu.VMEM((2, 2, 4, size_y // 2, quarter), F32),
            pltpu.VMEM((2, 2, size_x, 4, 1, quarter), F32),
            pltpu.VMEM((2, 2, size_x, 4, 1, quarter), F32),
            pltpu.VMEM((size_x // 2, 2, size_y, quarter), F32),
            pltpu.VMEM((ngy, ngx) + piece1, F32),
            pltpu.VMEM((ngy, ngx, 4) + piece1, F32),
            pltpu.VMEM((6, ngx) + block1, F32),
            pltpu.VMEM((ngx + 1,) + block1, F32),
            pltpu.VMEM((ngx + 2,) + block1, F32),
            pltpu.VMEM((7, ngx, size_p, quarter), F32),
            pltpu.VMEM((2, 2, size_y, quarter), F32),
            pltpu.VMEM((size_z, size_z), jnp.bfloat16),
            dma((3, 2)), dma((3, 2)), dma((2, 2)), dma((2, 2)),
            dma((3, most)), dma((3, most)), dma((4, most)), dma((4, most)),
        ],
        compiler_params=pltpu.CompilerParams(
            collective_id=0, has_side_effects=True, vmem_limit_bytes=62 * 1024 * 1024
        ),
    )(rhs, alpha, beta_x, beta_y, beta_z)


def solution(mesh):
    spec = P("gx", "gy", None)
    return jax.shard_map(
        functools.partial(on_device, mesh.shape["gx"], mesh.shape["gy"]),
        mesh=mesh,
        in_specs=(spec,) * 5,
        out_specs=(spec, spec),
        check_vma=False,
    )
```
